32 devices in a mesh: groups: 1, slab: 4 (over z), sub: 4 (over y, x), chan: 2 (over core).
Axes of the slice: x: 2, y: 2, z: 4, core: 2. Of those that a mesh axis runs over, the one named last changes fastest.
Arguments:
- coords: float32 [3, 16384], P(None, ('groups', 'slab', 'sub')), may hold values from 0 to 128
- features: bfloat16 [16384, 64], P(('groups', 'slab', 'sub'), 'chan'), may hold values from -6 to 6
- valid_count: int32 [128], P(('groups', 'slab', 'sub')), may hold values from 1 to 128
- pair_block: int32 [4, 4, 4, 4], P(('groups', 'slab')), may hold values from 0 to 7, as said below
- pair_brick: int32 [4, 4, 4, 4], P(('groups', 'slab')), may hold values from 0 to 16383, as said below
- pair_count: int32 [4, 4, 4], P(('groups', 'slab')), may hold values from 0 to 4, as said below
- geometry: bfloat16 [64, 128, 128, 128], P('chan', ('groups', 'slab', 'sub')), may hold values from -6 to 6
- encoder_first: float32 [3, 64], replicated, may hold values from -3.5 to 3.5
- encoder_bias: float32 [64], replicated, may hold values from -3 to 3
- encoder_second: float32 [64, 64], P(None, 'chan'), may hold values from -0.75 to 0.75
- decoder_first: float32 [3, 64], replicated, may hold values from -3.5 to 3.5
- decoder_bias: float32 [64], replicated, may hold values from -3 to 3
- decoder_second: float32 [64, 64], P(None, 'chan'), may hold values from -0.75 to 0.75
- spectral: bfloat16 [1024, 32, 64, 64], P(('slab', 'sub')), may hold values from -4.1875 to 4.1875
- cotangent: bfloat16 [16384, 64], P(('groups', 'slab', 'sub'), 'chan'), may hold values from -6 to 6
Outputs:
- decoded: bfloat16 [16384, 64], P(('groups', 'slab', 'sub'), 'chan')
- grad_encoder_first: float32 [3, 64], P('groups')
- grad_encoder_bias: float32 [64], P('groups')
- grad_encoder_second: float32 [64, 64], P('groups', 'chan')
- grad_decoder_first: float32 [3, 64], P('groups')
- grad_decoder_bias: float32 [64], P('groups')
- grad_decoder_second: float32 [64, 64], P('groups', 'chan')
- grad_spectral: bfloat16 [1024, 32, 64, 64], P(('groups', 'slab', 'sub'), None, 'chan')
The draws below stay inside these ranges and needn't reach their ends.
Inputs may be any that keep to these rules, and one draw needn't show every extreme that they name: `pair_block`: a point block of the source device. `pair_brick`: a grid block of the destination device. Slot r to destination d is live if r < pair_count; in every draw some device receives 4 live slots from every device of its slab.
All inputs are finite; a program needn't handle non-finite values.
Results may differ from the reference program's by a relative error of at most 0.0045.
Values may be sent and summed in bfloat16 or wider, within the bound.
No kernel may reach another device: no remote copies, remote signals or barrier semaphores. Data moves between devices by JAX's collectives and lax.ppermute only.
A program may use at most 320 MiB of HBM per device.

```python
import jax
import jax.numpy as jnp
from jax import lax

C = 64
H = 64
GI = 128
GJ = 128
GK = 128
MODES = 32
BLOCK = 128
BRICK = 8
CAP = 4
PB = 8
POINTS = 16384
JK = 1024
N_SLAB = 4
N_SUB = 4


def pattern_base(key):
    devices = N_SLAB * N_SUB
    row_key, column_key, block_key = jax.random.split(key, 3)
    centre_row = jax.random.randint(row_key, (devices * PB,), 2, GJ - 2)
    centre_column = jax.random.randint(column_key, (devices * PB,), 1, GK // BRICK - 1)
    blocks = jax.random.randint(block_key, (N_SLAB, N_SUB, N_SUB, CAP), 0, PB)
    blocks = blocks.at[0, 0, 0, 0].set(PB - 1).at[0, 0, 0, 1].set(0)
    return (centre_row, centre_column, blocks)


def draw_pair_block(key, part):
    centre_row, centre_column, blocks = pattern_base(key)
    return blocks.astype(jnp.int32)


def draw_pair_brick(key, part):
    centre_row, centre_column, blocks = pattern_base(key)
    key = jax.random.fold_in(key, 11)
    devices = N_SLAB * N_SUB
    planes = GI // devices
    row_key, column_key, layer_key = jax.random.split(key, 3)
    draw_shape = (N_SLAB, N_SUB, N_SUB, CAP)
    source = (jnp.arange(N_SLAB)[:, None] * N_SUB + jnp.arange(N_SUB)[None, :])[:, :, None, None]
    owner_block = source * PB + blocks
    row_values = centre_row[owner_block] + jax.random.randint(row_key, draw_shape, -2, 3)
    column_values = centre_column[owner_block] + jax.random.randint(column_key, draw_shape, -1, 2)
    layers = jax.random.randint(layer_key, draw_shape, 0, planes)
    bricks = (layers * GJ + row_values) * (GK // BRICK) + column_values
    top = planes * GJ * (GK // BRICK) - 1
    bricks = bricks.at[N_SLAB - 1, N_SUB - 1, N_SUB - 1, CAP - 1].set(top)
    bricks = bricks.at[N_SLAB - 1, N_SUB - 1, 0, 0].set(0)
    return bricks.astype(jnp.int32)


def draw_pair_count(key, part):
    key = jax.random.fold_in(key, 13)
    count_key, slab_key, sub_key = jax.random.split(key, 3)
    counts = jax.random.randint(count_key, (N_SLAB, N_SUB, N_SUB), 0, CAP + 1)
    slab_pick = jax.random.randint(slab_key, (), 0, N_SLAB)
    sub_pick = jax.random.randint(sub_key, (), 0, N_SUB)
    counts = counts.at[slab_pick, :, sub_pick].set(CAP)
    counts = counts.at[slab_pick, 0, (sub_pick + 1) % N_SUB].set(0)
    return counts.astype(jnp.int32)


def draw_valid_count(key, part):
    key = jax.random.fold_in(key, 17)
    count_key, pick_key = jax.random.split(key, 2)
    entries = N_SLAB * N_SUB * PB
    counts = jax.random.randint(count_key, (entries,), 1, BLOCK + 1)
    chosen = jax.random.randint(pick_key, (), 0, entries)
    counts = counts.at[chosen].set(BLOCK).at[(chosen + 1) % entries].set(1)
    return counts.astype(jnp.int32)


def draw_coords(key, part):
    centre_row, centre_column, blocks = pattern_base(key)
    key = jax.random.fold_in(key, 19)
    devices = N_SLAB * N_SUB
    planes = GI // devices
    slab_span = N_SUB * planes
    plane_key, row_key, column_key = jax.random.split(key, 3)
    draw_shape = (devices * PB, BLOCK)
    slab_of = (jnp.arange(devices * PB) // (PB * N_SUB)).astype(jnp.float32)[:, None]
    plane_axis = slab_of * slab_span + jax.random.uniform(plane_key, draw_shape, jnp.float32) * slab_span
    row_axis = centre_row.astype(jnp.float32)[:, None] + 0.5 + 1.5 * jax.random.normal(row_key, draw_shape, jnp.float32)
    row_axis = jnp.clip(row_axis, 0.0, GJ * 1.0)
    column_axis = centre_column.astype(jnp.float32)[:, None] * BRICK + 0.5 * BRICK + 4.0 * jax.random.normal(column_key, draw_shape, jnp.float32)
    column_axis = jnp.clip(column_axis, 0.0, GK * 1.0)
    return jnp.stack([plane_axis, row_axis, column_axis]).reshape(3, devices * PB * BLOCK)


def steps_of(rng, shape, cuts, least, top_value):
    factor_of, own = 1.0, jax.random.fold_in(rng, 6)
    for dim, shards_of in cuts:
        draws = jnp.exp(jax.random.uniform(jax.random.fold_in(own, dim), (shards_of,), jnp.float32, least / len(cuts), top_value / len(cuts)))
        factor_of = factor_of * jnp.repeat(draws, shape[dim] // shards_of).reshape([-1 if axis == dim else 1 for axis in range(len(shape))])
    return factor_of


def gaussian(own_key, shape, scale, limit, shards=(), kind=jnp.bfloat16):
    values = scale * jax.random.normal(own_key, shape, jnp.float32)
    if shards:
        values = values * steps_of(own_key, shape, shards, -0.22, 0.18)
    return jnp.clip(values, -limit, limit).astype(kind)


def setup_inputs(seed: int = 0, part: int = 0) -> dict:
    key_list = jax.random.split(jax.random.key(seed), 16)
    part_keys = jax.random.split(jax.random.fold_in(key_list[15], part), 16)
    return {
        "coords": draw_coords(jax.random.fold_in(jax.random.fold_in(key_list[15], part), 71), part),
        "features": gaussian(part_keys[1], (POINTS, C), 1.0, 6.0, ((0, 16), (1, 2))),
        "valid_count": draw_valid_count(jax.random.fold_in(jax.random.fold_in(key_list[15], part), 71), part),
        "pair_block": draw_pair_block(jax.random.fold_in(jax.random.fold_in(key_list[15], part), 71), part),
        "pair_brick": draw_pair_brick(jax.random.fold_in(jax.random.fold_in(key_list[15], part), 71), part),
        "pair_count": draw_pair_count(jax.random.fold_in(jax.random.fold_in(key_list[15], part), 71), part),
        "geometry": gaussian(part_keys[6], (C, GI, GJ, GK), 1.0, 6.0, ((0, 2), (1, 16))),
        "encoder_first": gaussian(key_list[7], (3, H), 3 ** -0.5, 3.5, (), jnp.float32),
        "encoder_bias": gaussian(key_list[8], (H,), 0.5, 3.0, (), jnp.float32),
        "encoder_second": gaussian(key_list[9], (H, C), H ** -0.5, 0.75, ((1, 2),), jnp.float32),
        "decoder_first": gaussian(key_list[10], (3, H), 3 ** -0.5, 3.5, (), jnp.float32),
        "decoder_bias": gaussian(key_list[11], (H,), 0.5, 3.0, (), jnp.float32),
        "decoder_second": gaussian(key_list[12], (H, C), H ** -0.5, 0.75, ((1, 2),), jnp.float32),
        "spectral": gaussian(key_list[13], (JK, MODES, C, C), 0.7, 4.1875, ((0, 16),)),
        "cotangent": gaussian(part_keys[14], (POINTS, C), 1.0, 6.0, ((0, 16), (1, 2))),
    }


RADIUS = 4.0
QUADRATURE = 0.0625
TOP_PRECISION = lax.Precision.HIGHEST

def basis(length, mode_count):
    positions = jnp.arange(length, dtype=jnp.float32)[:, None]
    halves = mode_count // 2
    degree = jnp.arange(halves, dtype=jnp.float32)[None, :]
    angle_cos = 2.0 * jnp.pi * degree * positions / length
    angle_sin = 2.0 * jnp.pi * (degree + 1.0) * positions / length
    weight_cos = jnp.where(degree == 0.0, jnp.sqrt(1.0 / length), jnp.sqrt(2.0 / length))
    return jnp.concatenate([jnp.cos(angle_cos) * weight_cos, jnp.sin(angle_sin) * jnp.sqrt(2.0 / length)], axis=1)

def brick_cells(first_plane, brick_index, count_row, count_column):
    per_row = count_column // BRICK
    layers = brick_index // (count_row * per_row)
    row_index = brick_index // per_row % count_row
    column = brick_index % per_row
    number = brick_index.shape[0]
    offsets = jnp.arange(BRICK, dtype=jnp.float32)[None, :]
    plane_axis = jnp.broadcast_to((first_plane + layers).astype(jnp.float32)[:, None] + 0.5, (number, BRICK))
    row_axis = jnp.broadcast_to(row_index.astype(jnp.float32)[:, None] + 0.5, (number, BRICK))
    column_axis = (column * BRICK).astype(jnp.float32)[:, None] + offsets + 0.5
    return jnp.stack([plane_axis, row_axis, column_axis], axis=1)

def kernel_values(weights, offset_cells):
    first_weight, first_bias, second_weight = weights
    hidden = jax.nn.gelu(jnp.einsum('sdpq,dh->spqh', offset_cells, first_weight, precision=TOP_PRECISION) + first_bias)
    return jnp.einsum('spqh,hc->spqc', hidden, second_weight, precision=TOP_PRECISION)

def encode_slots(weights, coords, features, point_weight, blocks, cell_points, live_mask):
    points = jnp.take(coords, blocks, axis=0)
    offset_cells = (cell_points[:, :, None, :] - points[:, :, :, None]) / RADIUS
    kernel = kernel_values(weights, offset_cells)
    sources = jnp.take(features, blocks, axis=0) * jnp.take(point_weight, blocks, axis=0)[:, :, None]
    sources = sources * live_mask[:, None, None]
    return jnp.einsum('spqc,spc->csq', kernel, sources, precision=TOP_PRECISION)

def decode_slots(weights, coords, blocks, cell_points, live_mask, bricks, inside):
    points = jnp.take(coords, blocks, axis=0)
    offset_cells = (points[:, :, :, None] - cell_points[:, :, None, :]) / RADIUS
    kernel = kernel_values(weights, offset_cells)
    scaled = bricks * (live_mask / BRICK)[None, :, None]
    contrib = jnp.einsum('spqc,csq->spc', kernel, scaled, precision=TOP_PRECISION)
    owner_map = (blocks[:, None] == jnp.arange(inside.shape[0], dtype=jnp.int32)[None, :]).astype(jnp.float32)
    collected_rows = jnp.einsum('sb,spc->bpc', owner_map, contrib, precision=TOP_PRECISION)
    return collected_rows * inside[:, :, None]

def analysis(field, tables):
    first_axis_table, table_j, table_k = tables
    transformed = jnp.einsum('cijk,kn->cijn', field, table_k, precision=TOP_PRECISION)
    transformed = jnp.einsum('cijn,jm->cimn', transformed, table_j, precision=TOP_PRECISION)
    return jnp.einsum('cimn,il->clmn', transformed, first_axis_table, precision=TOP_PRECISION)

def synthesis(modes, tables):
    first_axis_table, table_j, table_k = tables
    transformed = jnp.einsum('clmn,il->cimn', modes, first_axis_table, precision=TOP_PRECISION)
    transformed = jnp.einsum('cimn,jm->cijn', transformed, table_j, precision=TOP_PRECISION)
    return jnp.einsum('cijn,kn->cijk', transformed, table_k, precision=TOP_PRECISION)

def mix_modes(weights_five, spectral_factor):

    def one_row(row_number):
        weight_section = weights_five[row_number].astype(jnp.float32)
        return jnp.einsum('nlcd,cln->dln', weight_section, spectral_factor[:, :, row_number, :], precision=TOP_PRECISION)
    stacked = lax.map(one_row, jnp.arange(MODES, dtype=jnp.int32))
    return stacked.transpose(1, 2, 0, 3)

def mix_back(weights_five, grad_mixed):

    def one_row(row_number):
        weight_section = weights_five[row_number].astype(jnp.float32)
        return jnp.einsum('nlcd,dln->cln', weight_section, grad_mixed[:, :, row_number, :], precision=TOP_PRECISION)
    stacked = lax.map(one_row, jnp.arange(MODES, dtype=jnp.int32))
    return stacked.transpose(1, 2, 0, 3)

def spectral_grad(spectral_factor, grad_mixed):

    def one_row(row_number):
        outer_products = jnp.einsum('cln,dln->nlcd', spectral_factor[:, :, row_number, :], grad_mixed[:, :, row_number, :], precision=TOP_PRECISION)
        return outer_products.astype(jnp.bfloat16)
    return lax.map(one_row, jnp.arange(MODES, dtype=jnp.int32))

def total_over(stacked):
    return lax.optimization_barrier(jnp.sum(stacked, axis=0))

def reference(coords, features, valid_count, pair_block, pair_brick, pair_count, geometry, encoder_first, encoder_bias, encoder_second, decoder_first, decoder_bias, decoder_second, spectral, cotangent):
    devices = N_SLAB * N_SUB
    planes = GI // devices
    slot_count = N_SUB * CAP
    channel_count = geometry.shape[0]
    coords_dev = coords.reshape(3, devices, PB, BLOCK).transpose(1, 2, 0, 3)
    feats_dev = features.astype(jnp.float32).reshape(devices, PB, BLOCK, channel_count)
    inside = (jnp.arange(BLOCK, dtype=jnp.int32)[None, :] < valid_count[:, None]).astype(jnp.float32).reshape(devices, PB, BLOCK)
    blocks = pair_block.reshape(devices, slot_count)
    bricks = pair_brick.reshape(devices, slot_count)
    target = jnp.arange(slot_count, dtype=jnp.int32) // CAP
    limits = pair_count.reshape(devices, N_SUB)[:, target]
    live_mask = ((jnp.arange(slot_count, dtype=jnp.int32) % CAP)[None, :] < limits).astype(jnp.float32)
    slab_of = jnp.arange(devices, dtype=jnp.int32) // N_SUB
    first_plane = (slab_of[:, None] * N_SUB + target[None, :]) * planes
    cell_points = brick_cells(first_plane.reshape(-1), bricks.reshape(-1), GJ, GK).reshape(devices, slot_count, 3, BRICK)
    per_row = GK // BRICK
    plane_at = (first_plane + bricks // (GJ * per_row)).reshape(-1)
    row_at = (bricks // per_row % GJ).reshape(-1)
    column_at = (bricks % per_row).reshape(-1)
    encoder_weights = (encoder_first, encoder_bias, encoder_second)
    decoder_weights = (decoder_first, decoder_bias, decoder_second)
    grid_five = (channel_count, GI, GJ, per_row, BRICK)

    def encode_device(inputs):
        coords_one, feats_one, inside_one, blocks_one, cells_one, live_one = inputs
        return encode_slots(encoder_weights, coords_one, feats_one, inside_one * QUADRATURE, blocks_one, cells_one, live_one)
    partials = lax.map(encode_device, (coords_dev, feats_dev, inside, blocks, cell_points, live_mask))
    rounded = lax.optimization_barrier(partials.astype(jnp.bfloat16)).astype(jnp.float32)
    scattered_values = rounded.transpose(1, 0, 2, 3).reshape(channel_count, devices * slot_count, BRICK)
    encoded = jnp.zeros(grid_five, jnp.float32).at[:, plane_at, row_at, column_at, :].add(scattered_values)
    latent = (geometry.astype(jnp.float32) + encoded.reshape(geometry.shape)).astype(jnp.bfloat16)
    latent_wide = latent.astype(jnp.float32)
    tables = (basis(GI, MODES), basis(GJ, MODES), basis(GK, MODES))
    spectral_factor = analysis(latent_wide, tables)
    weights_five = spectral.reshape(MODES, MODES, MODES, channel_count, channel_count)
    mixed_modes = mix_modes(weights_five, spectral_factor)
    preact = synthesis(mixed_modes, tables) + latent_wide
    operator_out = jax.nn.gelu(preact).astype(jnp.bfloat16)
    read_bricks = operator_out.reshape(grid_five)[:, plane_at, row_at, column_at, :].astype(jnp.float32)
    read_bricks = read_bricks.reshape(channel_count, devices, slot_count, BRICK).transpose(1, 0, 2, 3)
    grad_points = cotangent.astype(jnp.float32).reshape(devices, PB, BLOCK, channel_count)

    def decode_device(inputs):
        coords_one, blocks_one, cells_one, live_one, inside_one, reads_one, grad_one = inputs

        def evaluate(weights, bricks_in):
            return decode_slots(weights, coords_one, blocks_one, cells_one, live_one, bricks_in, inside_one)
        values, pull = jax.vjp(evaluate, decoder_weights, reads_one)
        grad_weights, grad_reads = pull(grad_one)
        return (values, grad_weights, grad_reads)
    decoded_dev, decoder_grads, read_grads = lax.map(decode_device, (coords_dev, blocks, cell_points, live_mask, inside, read_bricks, grad_points))
    decoded = decoded_dev.reshape(devices * PB * BLOCK, channel_count).astype(jnp.bfloat16)
    spread_grads = read_grads.transpose(1, 0, 2, 3).reshape(channel_count, devices * slot_count, BRICK)
    grad_out = jnp.zeros(grid_five, jnp.float32).at[:, plane_at, row_at, column_at, :].add(spread_grads).reshape(geometry.shape)
    grad_preact = jax.vjp(jax.nn.gelu, preact)[1](grad_out)[0]
    grad_mixed = analysis(grad_preact, tables)
    grad_spectral = spectral_grad(spectral_factor, grad_mixed).reshape(MODES * MODES, MODES, channel_count, channel_count)
    spectral_factor_gradient = mix_back(weights_five, grad_mixed)
    grad_latent = grad_preact + synthesis(spectral_factor_gradient, tables)
    back_bricks = grad_latent.reshape(grid_five)[:, plane_at, row_at, column_at, :]
    back_bricks = back_bricks.reshape(channel_count, devices, slot_count, BRICK).transpose(1, 0, 2, 3)

    def encode_back(inputs):
        coords_one, feats_one, inside_one, blocks_one, cells_one, live_one, back_one = inputs

        def evaluate(weights):
            return encode_slots(weights, coords_one, feats_one, inside_one * QUADRATURE, blocks_one, cells_one, live_one)
        pull = jax.vjp(evaluate, encoder_weights)[1]
        return pull(back_one)[0]
    encoder_grads = lax.map(encode_back, (coords_dev, feats_dev, inside, blocks, cell_points, live_mask, back_bricks))
    encoder_sums = jax.tree.map(total_over, encoder_grads)
    decoder_sums = jax.tree.map(total_over, decoder_grads)
    return (decoded, encoder_sums[0], encoder_sums[1], encoder_sums[2], decoder_sums[0], decoder_sums[1], decoder_sums[2], grad_spectral)
```

```python
import functools

import jax
import jax.numpy as jnp
import numpy as np
from jax import lax
from jax.experimental import pallas as pl
from jax.experimental.pallas import tpu as pltpu
from jax.sharding import PartitionSpec as P

MODES = 32
BLOCK = 128
BRICK = 8
CAP = 4
RADIUS = 4.0
QUADRATURE = 0.0625
ROWS = 48

F32 = jnp.float32
BF16 = jnp.bfloat16
MIB = 1 << 20

NN = (((1,), (0,)), ((), ()))
NT = (((1,), (1,)), ((), ()))
TN = (((0,), (0,)), ((), ()))


def dot(a, b, dims=NN):
    return lax.dot_general(a, b, dims, preferred_element_type=F32)


def raw_basis(length):
    half = MODES // 2
    n = np.arange(length)[:, None]
    m = np.arange(half)[None, :]
    values = np.concatenate(
        [np.cos(2 * np.pi * m * n / length), np.sin(2 * np.pi * (m + 1) * n / length)], axis=1
    )
    norm = np.full(MODES, np.sqrt(2.0 / length))
    norm[0] = np.sqrt(1.0 / length)
    return values, norm


def halves(values):
    high = np.asarray(values, np.float32).astype(jnp.bfloat16)
    low = (np.asarray(values, np.float64) - high.astype(np.float64)).astype(jnp.bfloat16)
    return high, low


def split(value):
    high = value.astype(BF16).astype(F32)
    return high, value - high


def gelu_pair(x):
    a = 0.7978845608028654
    b = a * 0.044715
    x2 = x * x
    t = jnp.tanh(x * (a + b * x2))
    half = 0.5 + 0.5 * t
    slope = half + (0.5 * x) * (1.0 - t * t) * (a + (3.0 * b) * x2)
    return x * half, slope


def smem():
    return pl.BlockSpec(memory_space=pltpu.SMEM)


def vmem():
    return pl.BlockSpec(memory_space=pltpu.VMEM)


def params(mib):
    return pltpu.CompilerParams(vmem_limit_bytes=mib * MIB)


def cost(flops, nbytes):
    return pl.CostEstimate(flops=int(flops), bytes_accessed=int(nbytes), transcendentals=0)


def slot_offsets(s, cell, xs):
    return [cell[d, s] - xs[d : d + 1, :] for d in range(3)]


def slot_mask(s, b, live, count, weight):
    lanes = lax.broadcasted_iota(jnp.int32, (1, BLOCK), 1)
    return jnp.where(lanes < count[b], weight, 0.0) * live[s]


def net_kernel(
    sign, weight, keep, slots, blk, cell, live, count, x_ref, f_ref, w1_ref, w2_ref, *rest
):
    if keep:
        g_ref, slope_ref, part_ref, hid_all, part = rest
    else:
        crow_ref, g_ref, slope_ref, part_ref, hid_all, part = rest
    chan = f_ref.shape[0]
    hidden = w2_ref.shape[0]
    wide = BRICK * hidden
    part[...] = jnp.zeros_like(part)

    def step(s, carry):
        b = blk[s]
        at = pl.multiple_of(b * BLOCK, BLOCK)
        xs = x_ref[:, pl.ds(at, BLOCK)]
        mask = slot_mask(s, b, live, count, weight)
        f = (f_ref[:, pl.ds(at, BLOCK)].astype(F32) * mask).astype(BF16)
        e = slot_offsets(s, cell, xs)
        base = w1_ref[0] * e[0] + w1_ref[1] * e[1] + w1_ref[2] * e[2]
        base = w1_ref[3] + sign * base
        row = pl.multiple_of(s * wide, wide)
        hrow = row if keep else 0
        for q in range(BRICK):
            value, slope = gelu_pair(base + (sign * q) * w1_ref[2])
            hid_all[pl.ds(hrow + q * hidden, hidden), :] = value.astype(BF16)
            slope_ref[pl.ds(row + q * hidden, hidden), :] = slope.astype(BF16)
        g = dot(hid_all[pl.ds(hrow, wide), :], f, NT)
        g_ref[pl.ds(row, wide), :] = g.astype(BF16)
        summed = jnp.sum(g.reshape(BRICK, hidden, chan) * w2_ref[...][None], axis=1)
        part[pl.ds(pl.multiple_of(s * BRICK, BRICK), BRICK), 0:chan] = summed
        return carry

    lax.fori_loop(0, slots, step, 0)
    turned = jnp.transpose(part[...])[0:chan, :]
    if keep:
        part_ref[...] = turned
    else:
        message = jnp.concatenate([turned, crow_ref[...]], axis=0).astype(BF16)

        def copy(i, carry):
            part_ref[i] = message
            return carry

        lax.fori_loop(0, part_ref.shape[0], copy, 0)


def back_kernel(sign, weight, decode, slots, blk, cell, live, count, *rest):
    if decode:
        (x_ref, f_ref, w1_ref, w2_ref, g_ref, slope_ref, gp_ref, hid_ref,
         out_ref, dec_ref, m_ref, turn, dec) = rest
        gp = gp_ref[...]
        dec[...] = jnp.zeros_like(dec)
    else:
        x_ref, f_ref, w1_ref, w2_ref, g_ref, slope_ref, own_ref, recv_ref, out_ref, m_ref, turn = rest
        gp = own_ref[...] + jnp.sum(recv_ref[...].astype(F32), axis=0)
    chan = f_ref.shape[0]
    hidden = w2_ref.shape[0]
    wide = BRICK * hidden
    cells = gp.shape[1]
    turn[...] = jnp.transpose(
        jnp.concatenate([gp, jnp.zeros((128 - chan, cells), F32)], axis=0)
    )

    def step(s, carry):
        acc, grad2 = carry
        b = blk[s]
        at = pl.multiple_of(b * BLOCK, BLOCK)
        xs = x_ref[:, pl.ds(at, BLOCK)]
        mask = slot_mask(s, b, live, count, weight)
        f = (f_ref[:, pl.ds(at, BLOCK)].astype(F32) * mask).astype(BF16)
        e = slot_offsets(s, cell, xs)
        row = pl.multiple_of(s * wide, wide)
        gps = turn[pl.ds(pl.multiple_of(s * BRICK, BRICK), BRICK), 0:chan]
        for q in range(BRICK):
            line = gps[q : q + 1, :]
            m_ref[q * hidden : (q + 1) * hidden, :] = (w2_ref[...] * line).astype(BF16)
            grad2 = grad2 + line * g_ref[pl.ds(row + q * hidden, hidden), :].astype(F32)
        back = dot(m_ref[...], f)
        sum0 = jnp.zeros((hidden, BLOCK), F32)
        sum1 = jnp.zeros((hidden, BLOCK), F32)
        for q in range(BRICK):
            value = back[q * hidden : (q + 1) * hidden, :] * slope_ref[
                pl.ds(row + q * hidden, hidden), :
            ].astype(F32)
            sum0 = sum0 + value
            if q:
                sum1 = sum1 + float(q) * value
        scale = sign / RADIUS
        acc = (
            acc[0] + sum0 * (e[0] * scale),
            acc[1] + sum0 * (e[1] * scale),
            acc[2] + (sum0 * (e[2] * scale) + sum1 * scale),
            acc[3] + sum0,
        )
        if decode:
            inside = slot_mask(s, b, live, count, 1.0 / BRICK)
            value = dot(m_ref[...], hid_ref[pl.ds(row, wide), :], TN)
            dec[b] = dec[b] + value * inside
        return acc, grad2

    zero = jnp.zeros((hidden, BLOCK), F32)
    acc, grad2 = lax.fori_loop(
        0, slots, step, ((zero,) * 4, jnp.zeros((hidden, chan), F32))
    )
    sums = [jnp.sum(a, axis=1, keepdims=True) for a in acc]
    packed = jnp.concatenate(
        [grad2] + sums + [jnp.zeros((hidden, 128 - chan - 4), F32)], axis=1
    )
    out_ref[...] = jnp.transpose(packed)[0 : chan + 8, :]
    if decode:
        for b in range(dec.shape[0]):
            dec_ref[:, b * BLOCK : (b + 1) * BLOCK] = dec[b].astype(BF16)


def dense_kernel(planes, me, held, x_ref, fk_ref, lh_ref, ll_ref, perm_ref, out_ref, gb_ref, th, tl):
    p = pl.program_id(0)
    chan = x_ref.shape[0]
    length = x_ref.shape[2]
    for group in range(chan // 4):
        a = jnp.concatenate([x_ref[4 * group + i, 0] for i in range(4)], axis=1)
        t = dot(a, fk_ref[...])
        high, low = split(t[:, 0:128] + t[:, 128:256])
        rows = pl.ds(pl.multiple_of(p * length, length), length)
        th[rows, group * 128 : (group + 1) * 128] = high.astype(BF16)
        tl[rows, group * 128 : (group + 1) * 128] = low.astype(BF16)

    @pl.when(p == 0)
    def _():
        gb_ref[...] = jnp.zeros_like(gb_ref)

    cells = gb_ref.shape[2]

    def slot(t, carry):
        @pl.when(held[0, t] == p)
        def _():
            row = held[1, t]
            first = pl.multiple_of((row // 16) * 16, 16)
            tile = x_ref[:, 0, pl.ds(first, 16), :].astype(F32)
            inside = lax.broadcasted_iota(jnp.int32, (1, 16, 128), 1) == row - first
            line = jnp.sum(jnp.where(inside, tile, 0.0), axis=1).astype(BF16)
            u = t // CAP
            begin = (me[0] * CAP + t % CAP) * BRICK
            k = lax.broadcasted_iota(jnp.int32, (128, cells), 0)
            lane = lax.broadcasted_iota(jnp.int32, (128, cells), 1) - begin
            hot = (k == held[2, t] * BRICK + lane) & (lane >= 0) & (lane < BRICK)
            picked = dot(line, jnp.where(hot, 1.0, 0.0).astype(BF16))
            gb_ref[u] = gb_ref[u] + picked.astype(BF16)

        return carry

    lax.fori_loop(0, held.shape[1], slot, 0)

    @pl.when(p == planes - 1)
    def _():
        for piece in range(2):
            cols = slice(piece * 512, (piece + 1) * 512)
            r = dot(lh_ref[...], th[:, cols]) + dot(lh_ref[...], tl[:, cols])
            r = (r + dot(ll_ref[...], th[:, cols])).astype(BF16)
            th[0 : r.shape[0], cols] = r
        rows = out_ref.shape[0]
        out_ref[...] = dot(th[0:rows, :], perm_ref[...]).astype(BF16)


def prep_kernel(
    where, ag_ref, kx_ref, ix_ref, fj_ref, scale_ref, id_ref, gown_ref,
    bt_ref, dcoef_ref, lat_ref, p_ref,
):
    cells = ag_ref.shape[3]
    devices = ag_ref.shape[1]
    chan = p_ref.shape[0] // 2
    rows = bt_ref.shape[0]
    per = max(1, 256 // cells)
    width = per * cells
    piece = min(rows, 256)

    def place(i, carry):
        parts = [ag_ref[0, i * per + j, chan:ROWS, :].astype(F32) for j in range(per)]
        lines = jnp.concatenate(parts, axis=1)
        iota = lax.broadcasted_iota(jnp.int32, (128, width), 0).astype(F32)

        def hot(r):
            one = jnp.where(iota == lines[r : r + 1, :], 1.0, 0.0).astype(BF16)
            return jnp.concatenate([one, one], axis=0)

        tj = dot(fj_ref[...], hot(1))[0:1, :]
        hi, hk = hot(0), hot(2)
        at = pl.ds(pl.multiple_of(i * width, width), width)
        for r in range(rows // piece):
            rs = slice(r * piece, (r + 1) * piece)
            value = dot(kx_ref[rs, :], hk) * (dot(ix_ref[rs, :], hi) * tj)
            bt_ref[rs, at] = value.astype(BF16)
        for j in range(per):
            here = pl.ds(pl.multiple_of(i * width + j * cells, cells), cells)
            for c in range(2):
                p_ref[c * chan : (c + 1) * chan, here] = ag_ref[c, i * per + j, 0:chan, :]
        return carry

    lax.fori_loop(0, devices // per, place, 0)
    dcoef_ref[...] = dot(bt_ref[...], p_ref[...], NT) * scale_ref[...]
    subs = gown_ref.shape[0]
    encoded = jnp.zeros(lat_ref.shape, F32)
    for u in range(subs):
        lines = ag_ref[0, where[0] + u, chan:ROWS, :].astype(F32)
        same = cell_number(lines) == id_ref[...]
        here = ag_ref[where[1], where[0] + u, 0:chan, :]
        encoded = encoded + dot(here, jnp.where(same, 1.0, 0.0).astype(BF16), NT)
    geometry = jnp.sum(gown_ref[...].astype(F32), axis=0)
    lat_ref[...] = (geometry + encoded).astype(BF16).astype(F32)


def cell_number(lines):
    return lines[0:1, :] * 16384.0 + lines[1:2, :] * 128.0 + lines[2:3, :]


def send_cells(modes_rows, scale_row, bt_ref, sy_ref, turned):
    rows, devices2, chan, cells = bt_ref.shape[0], sy_ref.shape[0], sy_ref.shape[1], sy_ref.shape[2]
    value = jnp.transpose(modes_rows)[0 : 2 * chan, :] * scale_row
    high, low = split(value)
    turned[...] = jnp.concatenate([high, low], axis=0).astype(BF16)
    per = max(1, 256 // cells)
    width = per * cells

    def step(i, carry):
        at = pl.ds(pl.multiple_of(i * width, width), width)
        o = dot(turned[...], bt_ref[:, at])
        o = (o[0 : 2 * chan] + o[2 * chan :]).astype(BF16)
        for j in range(per):
            for c in range(2):
                sy_ref[(i * per + j) * 2 + c] = o[
                    c * chan : (c + 1) * chan, j * cells : (j + 1) * cells
                ]
        return carry

    lax.fori_loop(0, devices2 // 2 // per, step, 0, unroll=2)


def eight_mask():
    lane = lax.broadcasted_iota(jnp.int32, (8, 512), 1) // 64
    return jnp.where(lane == lax.broadcasted_iota(jnp.int32, (8, 512), 0), 1.0, 0.0)


def mix_kernel(
    chan_index, recv_ref, fi_ref, dcoef_ref, w_ref, bt_ref, scale_ref,
    sy_ref, coef_ref, coef, mix, turned,
):
    step = pl.program_id(0)
    steps = pl.num_programs(0)
    number = coef.shape[0] // MODES
    chan = coef_ref.shape[0] // 2

    @pl.when(step == 0)
    def _():
        mix[...] = jnp.zeros_like(mix)
        for c in range(2):
            if len(recv_ref.shape) == 4:
                got = recv_ref[:, c].astype(F32)
                got = got.reshape(got.shape[0] * got.shape[1], got.shape[2]).astype(BF16)
            else:
                got = recv_ref[c]
            x = dot(fi_ref[...], got)
            x = x[0:MODES] + x[MODES:]
            for n in range(number):
                coef[n * MODES : (n + 1) * MODES, c * chan : (c + 1) * chan] = x[
                    :, n * chan : (n + 1) * chan
                ]
        full = coef[:, 0 : 2 * chan] + dcoef_ref[...]
        coef[:, 0 : 2 * chan] = full
        coef[:, 2 * chan :] = jnp.zeros((coef.shape[0], 128 - 2 * chan), F32)
        coef_ref[...] = jnp.transpose(coef[...])[0 : 2 * chan, :]

    mask = eight_mask()
    here = w_ref.shape[0]
    for nn in range(here):
        for group in range(MODES // 8):
            rows = pl.ds(pl.multiple_of((step * here + nn) * MODES + group * 8, 8), 8)
            c8 = coef[rows, 0:64]
            c128 = jnp.concatenate([c8, c8], axis=1)
            big = jnp.concatenate([c128] * 4, axis=1) * mask
            high, low = split(big)
            left = jnp.concatenate([high, low], axis=0).astype(BF16)
            right = w_ref[nn, group * 8 : (group + 1) * 8].reshape(512, 64)
            o = dot(left, right)
            mix[rows, 0:64] = o[0:8] + o[8:16]

    @pl.when(step == steps - 1)
    def _():
        send_cells(mix[...], scale_ref[...], bt_ref, sy_ref, turned)


def mixback_kernel(
    chan_index, recv_ref, w_ref, bt_ref, column_ref, scale_ref,
    sy_ref, gm_ref, gm, mix, turned, g_ref,
):
    step = pl.program_id(0)
    steps = pl.num_programs(0)
    devices2, chan, cells = recv_ref.shape

    @pl.when(step == 0)
    def _():
        mix[...] = jnp.zeros_like(mix)
        gm[...] = jnp.zeros_like(gm)

        def place(i, carry):
            at = pl.ds(pl.multiple_of(i * cells, cells), cells)
            for c in range(2):
                g_ref[c * chan : (c + 1) * chan, at] = recv_ref[2 * i + c]
            return carry

        lax.fori_loop(0, devices2 // 2, place, 0)
        gm[:, 0:64] = dot(bt_ref[...], g_ref[...], NT) * column_ref[...]
        gm_ref[...] = jnp.transpose(gm[...])[0:64, :]

    mask = eight_mask()
    here = w_ref.shape[0]
    for nn in range(here):
        for group in range(MODES // 8):
            rows = pl.ds(pl.multiple_of((step * here + nn) * MODES + group * 8, 8), 8)
            high, low = split(gm[rows, 0:64])
            left = jnp.concatenate([high, low], axis=0).astype(BF16)
            right = w_ref[nn, group * 8 : (group + 1) * 8].reshape(512, 64)
            o = dot(left, right, NT)
            o = (o[0:8] + o[8:16]) * mask
            o = (o[:, 0:128] + o[:, 128:256]) + (o[:, 256:384] + o[:, 384:512])
            mix[rows, 0:64] = o[:, 0:64] + o[:, 64:128]

    @pl.when(step == steps - 1)
    def _():
        send_cells(mix[...], scale_ref[...], bt_ref, sy_ref, turned)


def point_kernel(recv_ref, lat_ref, rg_ref, g_ref, b_ref):
    preact = lat_ref[...] + jnp.sum(recv_ref[...].astype(F32), axis=0)
    value, slope = gelu_pair(preact)
    b_ref[...] = value.astype(BF16).astype(F32)
    g = (slope * rg_ref[...]).astype(BF16)

    def copy(i, carry):
        g_ref[i] = g
        return carry

    lax.fori_loop(0, g_ref.shape[0], copy, 0)


def own_kernel(where, ag_ref, recv_ref, id_ref, out_ref):
    chan = recv_ref.shape[1]
    total = jnp.zeros(out_ref.shape, F32)
    for u in range(where.shape[0] - 2):
        lines = ag_ref[0, where[0] + u, chan:ROWS, :].astype(F32)
        same = jnp.where(cell_number(lines) == id_ref[...], 1.0, 0.0).astype(BF16)
        total = total + dot(recv_ref[(where[0] + u) * 2 + where[1]], same, NT)
    out_ref[...] = total


def outer_kernel(chan_index, c_own, c_far, g_own, g_far, out_ref):
    mine = pl.program_id(0) == chan_index[0]
    coef = jnp.where(mine, c_own[...], c_far[...])
    grad = jnp.transpose(jnp.where(mine, g_own[...], g_far[...]))
    width = coef.shape[1]
    for x in range(width):
        value = coef[:, x : x + 1] * grad[x : x + 1, :]
        out_ref[x // MODES, x % MODES] = value.astype(BF16)


def tables(planes, devices, count_j, count_k):
    count_i = planes * devices
    raw_i, norm_i = raw_basis(count_i)
    raw_j, norm_j = raw_basis(count_j)
    raw_k, norm_k = raw_basis(count_k)
    fk_high, fk_low = halves(raw_k * norm_k)
    fk = np.zeros((4, count_k, 2, 4, MODES), jnp.bfloat16)
    for c in range(4):
        fk[c, :, 0, c] = fk_high
        fk[c, :, 1, c] = fk_low
    fj_high, fj_low = halves(raw_j * norm_j)
    left = np.zeros((2, MODES, planes, planes, count_j), jnp.bfloat16)
    for p in range(planes):
        left[0, :, p, p] = fj_high.T
        left[1, :, p, p] = fj_low.T
    left = left.reshape(2, MODES * planes, planes * count_j)
    fi_high, fi_low = halves(raw_i * norm_i)
    fi = np.concatenate([fi_high.T, fi_low.T], axis=0)

    def expand(raw, order):
        high, low = halves(raw)
        both = np.concatenate([high.T, low.T], axis=1)
        return np.repeat(both, MODES, axis=0) if order == "rep" else np.tile(both, (MODES, 1))

    kx = expand(raw_k, "rep")
    ix = expand(raw_i, "tile")
    fj_rows = np.concatenate([h.T for h in halves(raw_j)], axis=1)
    norm_nl = np.repeat(norm_k, MODES) * np.tile(norm_i, MODES)
    return {
        "fk": fk.reshape(4 * count_k, 8 * MODES),
        "lh": left[0],
        "ll": left[1],
        "fi": fi,
        "kx": kx,
        "ix": ix,
        "fj": fj_rows,
        "norm_nl": norm_nl.astype(np.float32),
        "norm_j": norm_j.astype(np.float32),
    }


def permutation(chan):
    perm = np.zeros((chan, MODES, MODES, chan), jnp.bfloat16)
    for c in range(chan):
        for n in range(MODES):
            perm[c, n, n, c] = 1
    return perm.reshape(chan * MODES, MODES * chan)


def body(
    coords,
    features,
    valid_count,
    pair_block,
    pair_brick,
    pair_count,
    geometry,
    encoder_first,
    encoder_bias,
    encoder_second,
    decoder_first,
    decoder_bias,
    decoder_second,
    spectral,
    cotangent,
):
    subs = lax.axis_size("sub")
    devices = lax.axis_size("slab") * subs
    every = ("slab", "sub", "chan")
    slab_index = lax.axis_index("slab")
    sub_index = lax.axis_index("sub")
    chan_index = lax.axis_index("chan")
    pair = slab_index * subs + sub_index
    blocks_here = valid_count.shape[0]
    chan, planes, count_j, count_k = geometry.shape
    points = features.shape[0]
    hidden = encoder_first.shape[1]
    slots = subs * CAP
    cells = slots * BRICK
    all_cells = devices * cells
    own = spectral.shape[0] // 2
    rows = own * MODES
    split_n = MODES // own
    tab = tables(planes, devices, count_j, count_k)
    per_row = count_k // BRICK

    blk = lax.dynamic_index_in_dim(pair_block[0], sub_index, 0, keepdims=False).reshape(slots)
    brick = lax.dynamic_index_in_dim(pair_brick[0], sub_index, 0, keepdims=False).reshape(slots)
    limits = lax.dynamic_index_in_dim(pair_count[0], sub_index, 0, keepdims=False)
    number = jnp.arange(slots, dtype=jnp.int32)
    target = number // CAP
    live = (number % CAP < jnp.repeat(limits, CAP)).astype(F32)

    def place(values):
        return values // (count_j * per_row), values // per_row % count_j, values % per_row

    layer, row, column = place(brick)
    plane = (slab_index * subs + target) * planes + layer
    cell = jnp.stack([plane, row, column * BRICK]).astype(F32) + 0.5
    lane_i = jnp.repeat(plane, BRICK)
    lane_j = jnp.repeat(row, BRICK)
    lane_k = jnp.repeat(column * BRICK, BRICK) + jnp.tile(jnp.arange(BRICK, dtype=jnp.int32), slots)
    coordinate_rows = jnp.concatenate(
        [jnp.stack([lane_i, lane_j, lane_k]).astype(F32), jnp.zeros((ROWS - chan - 3, cells), F32)]
    )
    own_id = (lane_i * 16384 + lane_j * 128 + lane_k).astype(F32)[:, None]
    held_brick = lax.dynamic_index_in_dim(pair_brick[0], sub_index, 1, keepdims=False).reshape(slots)
    held = jnp.stack(place(held_brick))
    where = jnp.concatenate(
        [jnp.stack([slab_index * subs, chan_index]), jnp.zeros((subs,), jnp.int32)]
    ).astype(jnp.int32)
    me = sub_index.astype(jnp.int32).reshape(1)
    core = chan_index.astype(jnp.int32).reshape(1)

    def first_layer(first, bias):
        stacked = jnp.concatenate([first / RADIUS, bias[None]], axis=0)
        return jnp.broadcast_to(stacked[:, :, None], (4, hidden, BLOCK))

    enc_w1 = first_layer(encoder_first, encoder_bias)
    dec_w1 = first_layer(decoder_first, decoder_bias)
    features_t = features.T
    cotangent_t = cotangent.T
    wide = BRICK * hidden

    def net(sign, weight, keep, f, w1, w2):
        hid_rows = slots * wide if keep else wide
        outs = [
            jax.ShapeDtypeStruct((slots * wide, chan), BF16),
            jax.ShapeDtypeStruct((slots * wide, BLOCK), BF16),
        ]
        args = [blk, cell, live, valid_count, coords, f, w1, w2]
        scratch = [pltpu.VMEM((cells, 128), F32)]
        if keep:
            outs.append(jax.ShapeDtypeStruct((chan, cells), F32))
            outs.append(jax.ShapeDtypeStruct((hid_rows, BLOCK), BF16))
        else:
            outs.append(jax.ShapeDtypeStruct((devices, ROWS, cells), BF16))
            args.append(coordinate_rows)
            scratch = [pltpu.VMEM((wide, BLOCK), BF16)] + scratch
        return pl.pallas_call(
            functools.partial(net_kernel, sign, weight, keep, slots),
            out_shape=outs,
            in_specs=[smem()] * 4 + [vmem()] * (len(args) - 4),
            out_specs=[vmem()] * len(outs),
            scratch_shapes=scratch,
            compiler_params=params(32),
            cost_estimate=cost(2e9, 8e6),
        )(*args)

    with jax.named_scope("encoder_points"):
        enc_g, enc_slope, message = net(
            1.0, QUADRATURE, False, features_t, enc_w1, encoder_second
        )
    with jax.named_scope("partials_all"):
        near = lax.all_to_all(message, ("slab", "sub"), 0, 0, tiled=True)
        gathered = lax.all_gather(near, "chan", axis=0)

    with jax.named_scope("dense_transform"):
        lanes = chan * MODES
        dense, held_values = pl.pallas_call(
            functools.partial(dense_kernel, planes),
            grid=(planes,),
            out_shape=[
                jax.ShapeDtypeStruct((MODES * planes, lanes), BF16),
                jax.ShapeDtypeStruct((subs, chan, cells), BF16),
            ],
            in_specs=[
                smem(),
                smem(),
                pl.BlockSpec((chan, 1, count_j, count_k), lambda p: (0, p, 0, 0)),
            ]
            + [vmem()] * 4,
            out_specs=[
                pl.BlockSpec((MODES * planes, lanes), lambda p: (0, 0)),
                pl.BlockSpec((subs, chan, cells), lambda p: (0, 0, 0)),
            ],
            scratch_shapes=[
                pltpu.VMEM((planes * count_j, lanes), BF16),
                pltpu.VMEM((planes * count_j, lanes), BF16),
            ],
            compiler_params=params(40),
            cost_estimate=cost(8e9, 1e7),
        )(
            me,
            held,
            geometry,
            jnp.asarray(tab["fk"]),
            jnp.asarray(tab["lh"]),
            jnp.asarray(tab["ll"]),
            jnp.asarray(permutation(chan)),
        )
    with jax.named_scope("dense_exchange"):
        dense = dense.reshape(MODES, planes, split_n, own * chan)
        dense = dense.transpose(0, 2, 1, 3).reshape(MODES * split_n, planes, own * chan)
        dense = lax.all_to_all(dense, every, 0, 0, tiled=True)
        dense = dense.reshape(devices, 2, planes, own * chan)
        if planes % 8:
            dense = dense.transpose(1, 0, 2, 3).reshape(2, devices * planes, own * chan)
    with jax.named_scope("held_exchange"):
        geometry_own = lax.all_to_all(held_values, "sub", 0, 0, tiled=True)

    with jax.named_scope("decoder_points"):
        dec_g, dec_slope, read_grads, dec_hid = net(
            -1.0, 1.0 / BRICK, True, cotangent_t, dec_w1, decoder_second
        )

    first_pair = (pair * 2 + chan_index) * own
    mode_j = first_pair // MODES
    kx = jnp.asarray(tab["kx"])
    norm_nl = jnp.asarray(tab["norm_nl"])
    if split_n > 1:
        begin = first_pair % MODES * MODES
        kx = lax.dynamic_slice_in_dim(kx, begin, rows, 0)
        norm_nl = lax.dynamic_slice_in_dim(norm_nl, begin, rows, 0)
    scale = norm_nl * lax.dynamic_index_in_dim(jnp.asarray(tab["norm_j"]), mode_j, 0, keepdims=False)
    scale_column, scale_row = scale[:, None], scale[None, :]
    fj = lax.dynamic_slice_in_dim(jnp.asarray(tab["fj"]), mode_j, 1, 0)
    fj = jnp.broadcast_to(fj, (16, fj.shape[1]))

    with jax.named_scope("cell_basis"):
        bt, sparse_coef, latent = pl.pallas_call(
            prep_kernel,
            out_shape=[
                jax.ShapeDtypeStruct((rows, all_cells), BF16),
                jax.ShapeDtypeStruct((rows, 2 * chan), F32),
                jax.ShapeDtypeStruct((chan, cells), F32),
            ],
            in_specs=[smem()] + [vmem()] * 7,
            out_specs=[vmem()] * 3,
            scratch_shapes=[pltpu.VMEM((2 * chan, all_cells), BF16)],
            compiler_params=params(40),
            cost_estimate=cost(5e9, 8e6),
        )(
            where,
            gathered,
            kx,
            jnp.asarray(tab["ix"][:rows]),
            fj,
            scale_column,
            own_id,
            geometry_own,
        )

    block_n = min(4, own)
    steps = own // block_n

    def weights_spec():
        return pl.BlockSpec(
            (block_n, MODES, 2 * chan, 2 * chan), lambda n, core: (core[0] * steps + n, 0, 0, 0)
        )

    def whole(array):
        rank = len(array.shape)
        return pl.BlockSpec(array.shape, lambda n, core: (0,) * rank)

    def mode_call(kernel, args, outs, scratch):
        specs = [weights_spec() if a is spectral else whole(a) for a in args]
        return pl.pallas_call(
            kernel,
            grid_spec=pltpu.PrefetchScalarGridSpec(
                num_scalar_prefetch=1,
                grid=(steps,),
                in_specs=specs,
                out_specs=[whole(o) for o in outs],
                scratch_shapes=scratch,
            ),
            out_shape=outs,
            compiler_params=params(40),
            cost_estimate=cost(4e9, 2.4e7),
        )(core, *args)

    readers = jax.ShapeDtypeStruct((2 * devices, chan, cells), BF16)
    by_mode = jax.ShapeDtypeStruct((2 * chan, rows), F32)
    with jax.named_scope("mix"):
        sent, coefficient = mode_call(
            mix_kernel,
            [dense, jnp.asarray(tab["fi"]), sparse_coef, spectral, bt, scale_row],
            [readers, by_mode],
            [
                pltpu.VMEM((rows, 128), F32),
                pltpu.VMEM((rows, 128), F32),
                pltpu.VMEM((4 * chan, rows), BF16),
            ],
        )
    with jax.named_scope("preact_exchange"):
        arrived = lax.all_to_all(sent, every, 0, 0, tiled=True)
    swap = [(0, 1), (1, 0)]
    with jax.named_scope("coefficient_swap"):
        coef_near = lax.dynamic_slice_in_dim(coefficient, chan_index * chan, chan, 0)
        coef_sent = lax.dynamic_slice_in_dim(coefficient, (1 - chan_index) * chan, chan, 0)
        coef_far = lax.ppermute(coef_sent, "chan", swap)

    with jax.named_scope("cell_values"):
        cell_grads, bricks = pl.pallas_call(
            point_kernel,
            out_shape=[readers, jax.ShapeDtypeStruct((chan, cells), F32)],
            in_specs=[vmem()] * 3,
            out_specs=[vmem()] * 2,
            compiler_params=params(16),
            cost_estimate=cost(1e6, 1e6),
        )(arrived, latent, read_grads)
    with jax.named_scope("cell_grads_all"):
        all_grads = lax.all_to_all(cell_grads, every, 0, 0, tiled=True)

    def back(sign, weight, decode, f, w1, w2, g, slope, *more):
        args = [blk, cell, live, valid_count, coords, f, w1, w2, g, slope, *more]
        outs = [jax.ShapeDtypeStruct((chan + 8, hidden), F32)]
        scratch = [pltpu.VMEM((wide, chan), BF16), pltpu.VMEM((cells, 128), F32)]
        if decode:
            outs.append(jax.ShapeDtypeStruct((chan, points), BF16))
            scratch.append(pltpu.VMEM((blocks_here, chan, BLOCK), F32))
        return pl.pallas_call(
            functools.partial(back_kernel, sign, weight, decode, slots),
            out_shape=outs,
            in_specs=[smem()] * 4 + [vmem()] * (len(args) - 4),
            out_specs=[vmem()] * len(outs),
            scratch_shapes=scratch,
            compiler_params=params(32),
            cost_estimate=cost(2e9, 8e6),
        )(*args)

    with jax.named_scope("decoder_back"):
        dec_grads, decoded = back(
            -1.0, 1.0 / BRICK, True, cotangent_t, dec_w1, decoder_second,
            dec_g, dec_slope, bricks, dec_hid,
        )

    with jax.named_scope("mix_back"):
        sent_back, grad_modes = mode_call(
            mixback_kernel,
            [all_grads, spectral, bt, scale_column, scale_row],
            [readers, by_mode],
            [
                pltpu.VMEM((rows, 128), F32),
                pltpu.VMEM((rows, 128), F32),
                pltpu.VMEM((4 * chan, rows), BF16),
                pltpu.VMEM((2 * chan, all_cells), BF16),
            ],
        )
    with jax.named_scope("latent_grad_exchange"):
        arrived_back = lax.all_to_all(sent_back, every, 0, 0, tiled=True)
    with jax.named_scope("grad_swap"):
        grad_far = lax.ppermute(grad_modes, "chan", swap)
    with jax.named_scope("own_cells"):
        own_grads = pl.pallas_call(
            own_kernel,
            out_shape=jax.ShapeDtypeStruct((chan, cells), F32),
            in_specs=[smem()] + [vmem()] * 3,
            out_specs=vmem(),
            compiler_params=params(16),
            cost_estimate=cost(1e8, 1e6),
        )(where, gathered, all_grads, own_id)

    with jax.named_scope("grad_spectral"):
        width = block_n * MODES

        def lanes_spec(height):
            return pl.BlockSpec((height, width), lambda h, n, core: (0, n))

        grad_spectral = pl.pallas_call(
            outer_kernel,
            grid_spec=pltpu.PrefetchScalarGridSpec(
                num_scalar_prefetch=1,
                grid=(2, steps),
                in_specs=[lanes_spec(chan)] * 2 + [lanes_spec(2 * chan)] * 2,
                out_specs=pl.BlockSpec(
                    (block_n, MODES, chan, 2 * chan), lambda h, n, core: (h * steps + n, 0, 0, 0)
                ),
            ),
            out_shape=jax.ShapeDtypeStruct((2 * own, MODES, chan, 2 * chan), BF16),
            compiler_params=params(32),
            cost_estimate=cost(1e7, 1.8e7),
        )(core, coef_near, coef_far, grad_modes, grad_far)

    with jax.named_scope("encoder_back"):
        (enc_grads,) = back(
            1.0, QUADRATURE, False, features_t, enc_w1, encoder_second,
            enc_g, enc_slope, own_grads, arrived_back,
        )
    with jax.named_scope("weight_sums"):
        both = jnp.concatenate([enc_grads, dec_grads], axis=1).astype(BF16)
        spread = jnp.broadcast_to(both[None], (devices,) + both.shape)
        total = jnp.sum(
            lax.all_to_all(spread, ("slab", "sub"), 0, 0, tiled=True).astype(F32), axis=0
        )
        small = total[chan:]
        small = small + lax.ppermute(small, "chan", swap)
    enc_second = total[:chan, :hidden].T
    dec_second = total[:chan, hidden:].T
    return (
        decoded.T,
        small[0:3, :hidden],
        small[3, :hidden],
        enc_second,
        small[0:3, hidden:],
        small[3, hidden:],
        dec_second,
        grad_spectral,
    )


def solution(mesh):
    placed = (
        P(None, ("groups", "slab", "sub")),
        P(("groups", "slab", "sub"), "chan"),
        P(("groups", "slab", "sub")),
        P(("groups", "slab"), None, None, None),
        P(("groups", "slab"), None, None, None),
        P(("groups", "slab"), None, None),
        P("chan", ("groups", "slab", "sub"), None, None),
        P(),
        P(),
        P(None, "chan"),
        P(),
        P(),
        P(None, "chan"),
        P(("slab", "sub"), None, None, None),
        P(("groups", "slab", "sub"), "chan"),
    )
    return jax.shard_map(
        body,
        mesh=mesh,
        in_specs=placed,
        out_specs=(
            P(("groups", "slab", "sub"), "chan"),
            P("groups", None),
            P("groups"),
            P("groups", "chan"),
            P("groups", None),
            P("groups"),
            P("groups", "chan"),
            P(("groups", "slab", "sub"), None, "chan", None),
        ),
        check_vma=False,
    )
```

```python
import functools

import jax
import jax.numpy as jnp
import numpy as np
from jax import lax
from jax.experimental import pallas as pl
from jax.experimental.pallas import tpu as pltpu
from jax.sharding import PartitionSpec as P

MODES = 32
BLOCK = 128
BRICK = 8
CAP = 4
RADIUS = 4.0
QUADRATURE = 0.0625

F32 = jnp.float32
BF16 = jnp.bfloat16
MIB = 1 << 20

NN = (((1,), (0,)), ((), ()))
NT = (((1,), (1,)), ((), ()))
TN = (((0,), (0,)), ((), ()))


def dot(a, b, dims=NN):
    return lax.dot_general(a, b, dims, preferred_element_type=F32)


def raw_basis(length):
    half = MODES // 2
    n = np.arange(length)[:, None]
    m = np.arange(half)[None, :]
    values = np.concatenate(
        [np.cos(2 * np.pi * m * n / length), np.sin(2 * np.pi * (m + 1) * n / length)], axis=1
    )
    norm = np.full(MODES, np.sqrt(2.0 / length))
    norm[0] = np.sqrt(1.0 / length)
    return values, norm


def halves(values):
    high = np.asarray(values, np.float32).astype(jnp.bfloat16)
    low = (np.asarray(values, np.float64) - high.astype(np.float64)).astype(jnp.bfloat16)
    return high, low


def split(value):
    high = value.astype(BF16).astype(F32)
    return high, value - high


def over(x, d):
    return x >> (d.bit_length() - 1) if d & (d - 1) == 0 else lax.div(x, d)


def modulo(x, d):
    return x & (d - 1) if d & (d - 1) == 0 else lax.rem(x, d)


def gelu_pair(x):
    a = 0.7978845608028654
    b = a * 0.044715
    x2 = x * x
    t = jnp.tanh(x * (a + b * x2))
    half = 0.5 + 0.5 * t
    slope = half + (0.5 * x) * (1.0 - t * t) * (a + (3.0 * b) * x2)
    return x * half, slope


VMEM_LIMIT = 62 * MIB


class Late:
    def __init__(self, source, target, sems, pieces, axis, held, ahead):
        self.source, self.target, self.sems, self.ahead = source, target, sems, ahead
        self.pieces, self.axis, self.ref = pieces, axis, held

    def copy(self, i):
        size = self.ref.shape[self.axis] // self.pieces
        if isinstance(i, int):
            piece = pl.ds(i * size, size)
        else:
            piece = pl.ds(pl.multiple_of(i * size, size), size)
        at = (slice(None),) * self.axis + (piece,)
        return pltpu.make_async_copy(self.source.at[at], self.target.at[at], self.sems.at[i])

    def start(self, i):
        self.copy(i).start()

    def wait(self, i):
        self.copy(i).wait()


def call(kernel, ins, outs, scratch=(), flops=1e9, nbytes=8e6):
    buffers, sems = [], []
    modes_in, modes_out = [m for _, m in ins], [m for _, m in outs]
    for array, mode in [*ins, *outs]:
        if mode == "raw":
            continue
        space = pltpu.SMEM if mode == "scalar" else pltpu.VMEM
        buffers.append(space(array.shape, array.dtype))
        sems.append(pltpu.SemaphoreType.DMA((mode[0] if isinstance(mode, tuple) else 1,)))

    def wrapped(*refs):
        arrays = refs[: len(ins) + len(outs)]
        rest = refs[len(ins) + len(outs) :]
        held, signals = rest[: len(buffers)], rest[len(buffers) : 2 * len(buffers)]
        more = rest[2 * len(buffers) :]
        objects, early, late, place = [], [], [], 0
        for i, (array, mode) in enumerate(zip(arrays, modes_in + modes_out)):
            if mode == "raw":
                objects.append(array)
                continue
            buffer, sem = held[place], signals[place]
            place += 1
            pieces, axis = mode if isinstance(mode, tuple) else (1, 0)
            source, target = (array, buffer) if i < len(ins) else (buffer, array)
            one = Late(source, target, sem, pieces, axis, buffer, i < len(ins))
            if isinstance(mode, tuple):
                objects.append(one)
                late.append((i, one))
            else:
                objects.append(buffer)
                early.append((i, pltpu.make_async_copy(source, target, sem.at[0])))
        for i, one in early:
            if i < len(ins):
                one.start()
        for i, one in late:
            if i < len(ins):
                for j in range(one.pieces):
                    one.start(j)
        for i, one in early:
            if i < len(ins):
                one.wait()
        kernel(*objects, *more)
        for i, one in early:
            if i >= len(ins):
                one.start()
        for i, one in early:
            if i >= len(ins):
                one.wait()
        for i, one in late:
            if i >= len(ins):
                for j in range(one.pieces):
                    one.wait(j)

    hbm = pl.BlockSpec(memory_space=pl.ANY)
    return pl.pallas_call(
        wrapped,
        out_shape=[jax.ShapeDtypeStruct(o.shape, o.dtype) for o, _ in outs],
        in_specs=[hbm] * len(ins),
        out_specs=[hbm] * len(outs),
        scratch_shapes=[*buffers, *sems, *scratch],
        compiler_params=pltpu.CompilerParams(vmem_limit_bytes=VMEM_LIMIT),
        cost_estimate=pl.CostEstimate(
            flops=int(flops), bytes_accessed=int(nbytes), transcendentals=0
        ),
    )(*[a for a, _ in ins])


class Slots:
    def __init__(self, refs, subs, planes, count_j, per_row):
        self.block_ref, self.brick_ref, self.count_ref, self.valid_ref = refs
        self.subs, self.planes = subs, planes
        self.count_j, self.per_row = count_j, per_row
        self.slots = subs * CAP
        self.slab = lax.axis_index("slab")
        self.me = lax.axis_index("sub")
        self.core = lax.axis_index("chan")

    def block(self, s):
        return self.block_ref[0, self.me, over(s, CAP), modulo(s, CAP)]

    def place(self, brick):
        row = modulo(over(brick, self.per_row), self.count_j)
        column = modulo(brick, self.per_row) * BRICK
        return over(brick, self.count_j * self.per_row), row, column

    def own(self, s):
        layer, row, column = self.place(self.brick_ref[0, self.me, over(s, CAP), modulo(s, CAP)])
        first = (self.slab * self.subs + over(s, CAP)) * self.planes
        return first + layer, row, column

    def held(self, t):
        return self.place(self.brick_ref[0, over(t, CAP), self.me, modulo(t, CAP)])

    def live(self, s):
        count = self.count_ref[0, self.me, over(s, CAP)]
        return jnp.where(modulo(s, CAP) < count, 1.0, 0.0)

    def valid(self, b):
        return self.valid_ref[b]

    def lines(self, which):
        cells = self.slots * BRICK
        lane = lax.broadcasted_iota(jnp.int32, (1, cells), 1)
        rows = [jnp.zeros((1, cells), jnp.int32)] * 3
        for s in range(self.slots):
            here = over(lane, BRICK) == s
            values = which(jnp.int32(s))
            rows = [jnp.where(here, v, r) for v, r in zip(values, rows)]
        rows[2] = rows[2] + modulo(lane, BRICK)
        return [r.astype(F32) for r in rows]


def cell_number(lines):
    return lines[0] * 16384.0 + lines[1] * 128.0 + lines[2]


def same_cells(column_lines, lines):
    number = cell_number(column_lines)
    tall = jnp.transpose(jnp.broadcast_to(number, (number.shape[1], number.shape[1])))
    return jnp.where(tall[:, 0:1] == cell_number(lines), 1.0, 0.0).astype(BF16)


def columns(first, bias, w1):
    hidden = first.shape[1]
    rows = jnp.concatenate(
        [first[...] * (1.0 / RADIUS), bias[...], jnp.zeros((124, hidden), F32)], axis=0
    )
    turned = jnp.transpose(rows)
    for d in range(4):
        w1[d] = jnp.broadcast_to(turned[:, d : d + 1], (hidden, BLOCK))


def second_layer(ref):
    return jnp.concatenate([ref[...], ref[...]], axis=1)


def slot_points(slots, s, x_ref):
    at = pl.multiple_of(slots.block(s) * BLOCK, BLOCK)
    xs = x_ref[:, pl.ds(at, BLOCK)]
    place = slots.own(s)
    return at, [(place[d].astype(F32) + 0.5) - xs[d : d + 1, :] for d in range(3)]


def slot_mask(slots, s, weight):
    lanes = lax.broadcasted_iota(jnp.int32, (1, BLOCK), 1)
    return jnp.where(lanes < slots.valid(slots.block(s)), weight, 0.0) * slots.live(s)


def slot_source(slots, s, at, f_ref, weight):
    return (f_ref[:, pl.ds(at, BLOCK)].astype(F32) * slot_mask(slots, s, weight)).astype(BF16)


def first_base(sign, e, w1):
    return w1[3] + sign * (w1[0] * e[0] + w1[1] * e[1] + w1[2] * e[2])


def spread_groups(me, values, outs):
    groups = len(outs)
    cells = values.shape[1]
    width = cells // groups
    lane = over(lax.broadcasted_iota(jnp.int32, (1, cells), 1), width)
    for k in range(groups):
        moved = pltpu.roll(values, (groups - k) % groups * width, 1) if k else values
        outs[k][...] = jnp.where(lane == me, moved, 0.0).astype(BF16)


def loop(slots, step, first, *arrays):
    each = slots // arrays[0].pieces

    def piece(i, carry):
        for array in arrays:
            if array.ahead:
                array.wait(i)
        for j in range(each):
            carry = step(i * each + j, carry)
        for array in arrays:
            if not array.ahead:
                array.start(i)
        return carry

    return lax.fori_loop(0, arrays[0].pieces, piece, first)


def net_kernel(sign, weight, keep, make, s0, s1, s2, s3, x_ref, f_ref, first, bias, second, *rest):
    slots = make((s0, s1, s2, s3))
    if keep:
        g, slope, hid, part_ref, w1, group = rest
    else:
        g, outs, (w1, group) = rest[0], rest[1:-2], rest[-2:]
    chan, hidden = second.shape
    wide = BRICK * hidden
    cells = slots.slots * BRICK
    columns(first, bias, w1)
    w2 = jnp.concatenate([second_layer(second)] * (BRICK // 2), axis=1)
    of_row = over(lax.broadcasted_iota(jnp.int32, (wide, 128), 0), hidden)
    at_lane = lax.broadcasted_iota(jnp.int32, (wide, 128), 1)
    group[...] = jnp.where(of_row == at_lane, 1.0, 0.0).astype(BF16)

    def step(s, part):
        at, e = slot_points(slots, s, x_ref)
        f = slot_source(slots, s, at, f_ref, weight)
        base = first_base(sign, e, w1)
        row = pl.multiple_of(s * wide, wide)
        values = []
        for q in range(BRICK):
            value, gradient = gelu_pair(base + (sign * q) * w1[2])
            values.append(value.astype(BF16))
            if keep:
                slope.ref[pl.ds(row + q * hidden, hidden), :] = gradient.astype(BF16)
        all_q = jnp.concatenate(values, axis=0)
        total = dot(f, all_q, NT)
        g.ref[pl.ds(pl.multiple_of(s * chan, chan), chan), :] = total.astype(BF16)
        if keep:
            hid.ref[pl.ds(row, wide), :] = all_q
        high, low = split(total * w2)
        both = jnp.concatenate([high, low], axis=0).astype(BF16)
        sums = dot(both, group[...])
        sums = sums[0:chan] + sums[chan:]
        if cells > 128:
            sums = jnp.concatenate([sums, jnp.zeros((chan, cells - 128), F32)], axis=1)
        return part + pltpu.roll(sums, s * BRICK, 1)

    kept = (g, slope, hid) if keep else (g,)
    part = loop(slots.slots, step, jnp.zeros((chan, cells), F32), *kept)
    if keep:
        part_ref[...] = part
    else:
        spread_groups(slots.me, part, outs)


def slope_kernel(sign, make, s0, s1, s2, s3, x_ref, first, bias, slope, w1):
    slots = make((s0, s1, s2, s3))
    columns(first, bias, w1)
    hidden = first.shape[1]
    wide = BRICK * hidden

    def step(s, carry):
        _, e = slot_points(slots, s, x_ref)
        base = first_base(sign, e, w1)
        row = pl.multiple_of(s * wide, wide)
        for q in range(BRICK):
            _, gradient = gelu_pair(base + (sign * q) * w1[2])
            slope.ref[pl.ds(row + q * hidden, hidden), :] = gradient.astype(BF16)
        return carry

    loop(slots.slots, step, 0, slope)


def back_kernel(sign, weight, decode, make, s0, s1, s2, s3, x_ref, f_ref, second, *rest):
    slots = make((s0, s1, s2, s3))
    if decode:
        gp_ref, g, slope, hid, out_ref, dec_ref, dec = rest
        gp = gp_ref[...]
        dec[...] = jnp.zeros_like(dec)
    else:
        own_ref, recv_ref, g, slope, out_ref = rest
        gp = own_ref[...] + jnp.sum(recv_ref[...].astype(F32), axis=0)
    chan, hidden = second.shape
    wide = BRICK * hidden
    cells = gp.shape[1]
    w2 = second_layer(second)
    left_half = lax.broadcasted_iota(jnp.int32, (1, 2 * hidden), 1) < hidden

    def step(s, carry):
        acc, grad2 = carry
        at, e = slot_points(slots, s, x_ref)
        f = slot_source(slots, s, at, f_ref, weight)
        row = pl.multiple_of(s * wide, wide)
        gps = pltpu.roll(gp, cells - s * BRICK, 1)
        gs = g.ref[pl.ds(pl.multiple_of(s * chan, chan), chan), :].astype(F32)
        m = []
        for i in range(BRICK // 2):
            both = jnp.where(left_half, gps[:, 2 * i : 2 * i + 1], gps[:, 2 * i + 1 : 2 * i + 2])
            m.append(w2 * both)
            grad2 = grad2 + gs[:, 2 * i * hidden : 2 * (i + 1) * hidden] * both
        m = jnp.concatenate(m, axis=1)
        back = dot(jnp.transpose(m).astype(BF16), f)
        sum0 = jnp.zeros((hidden, BLOCK), F32)
        sum1 = jnp.zeros((hidden, BLOCK), F32)
        for q in range(BRICK):
            value = back[q * hidden : (q + 1) * hidden, :] * slope.ref[
                pl.ds(row + q * hidden, hidden), :
            ].astype(F32)
            sum0 = sum0 + value
            if q:
                sum1 = sum1 + float(q) * value
        scale = sign / RADIUS
        acc = (
            acc[0] + sum0 * (e[0] * scale),
            acc[1] + sum0 * (e[1] * scale),
            acc[2] + (sum0 * (e[2] * scale) + sum1 * scale),
            acc[3] + sum0,
        )
        if decode:
            value = dot(m.astype(BF16), hid.ref[pl.ds(row, wide), :])
            b = slots.block(s)
            dec[b] = dec[b] + value * slot_mask(slots, s, 1.0 / BRICK)
        return acc, grad2

    zero = jnp.zeros((hidden, BLOCK), F32)
    kept = (g, slope, hid) if decode else (g, slope)
    acc, grad2 = loop(
        slots.slots, step, ((zero,) * 4, jnp.zeros((chan, 2 * hidden), F32)), *kept
    )
    sums = [jnp.sum(a, axis=1, keepdims=True) for a in acc]
    packed = jnp.concatenate(sums + [jnp.zeros((hidden, 124), F32)], axis=1)
    out_ref[0:chan, :] = grad2[:, 0:hidden] + grad2[:, hidden : 2 * hidden]
    out_ref[chan : chan + 8, :] = jnp.transpose(packed)[0:8, :]
    if decode:
        for b in range(dec.shape[0]):
            dec_ref[:, b * BLOCK : (b + 1) * BLOCK] = dec[b].astype(BF16)


def sparse_factors(slots, planes_modes, part, lines, kx_ref, fj_ref):
    chan, cells = part.shape
    lanes = kx_ref.shape[1]
    planes = planes_modes // MODES
    iota = lax.broadcasted_iota(jnp.int32, (128, cells), 0).astype(F32)

    def hot(line):
        one = jnp.where(iota == line, 1.0, 0.0).astype(BF16)
        return jnp.concatenate([one, one], axis=0)

    plane = lax.broadcasted_iota(jnp.int32, (planes_modes, cells), 0)
    here = modulo(plane, planes).astype(F32) == lines[0]
    high, low = split(jnp.where(here, dot(fj_ref[...], hot(lines[1])), 0.0))
    left = jnp.concatenate([high, high, low], axis=1).astype(BF16)
    turned = jnp.transpose(jnp.concatenate([part, jnp.zeros((128 - chan, cells), F32)], axis=0))
    turned = turned[:, 0:chan]
    four = jnp.concatenate([turned] * (128 // chan), axis=1)
    value = dot(hot(lines[2]), kx_ref[...], TN) * jnp.concatenate([four] * (lanes // 128), axis=1)
    high, low = split(value)
    return left, jnp.concatenate([high, low, high], axis=0).astype(BF16)


def dense_kernel(subs, make, s0, s1, s2, s3, fk_ref, fj_ref, *rest):
    got, (x, lh, ll, perm, kx), (out_ref, *lats), (th, tl) = (
        rest[:subs], rest[subs : subs + 5], rest[subs + 5 : -2], rest[-2:]
    )
    slots = make((s0, s1, s2, s3))
    chan, planes, length = x.ref.shape[0:3]
    cells = got[0].shape[1]

    def plane(p, carry):
        rows = pl.ds(pl.multiple_of(p * length, length), length)
        x.wait(p)
        for group in range(chan // 4):
            a = jnp.concatenate([x.ref[4 * group + i, p] for i in range(4)], axis=1)
            t = dot(a, fk_ref[...])
            high, low = split(t[:, 0:128] + t[:, 128:256])
            th[rows, group * 128 : (group + 1) * 128] = high.astype(BF16)
            tl[rows, group * 128 : (group + 1) * 128] = low.astype(BF16)
        return carry

    lax.fori_loop(0, planes, plane, 0)
    lh.wait(0)
    ll.wait(0)
    count = out_ref.shape[0]
    for piece in range(4):
        cols = slice(piece * 256, (piece + 1) * 256)
        r = dot(lh.ref[...], th[:, cols]) + dot(lh.ref[...], tl[:, cols])
        high, low = split(r + dot(ll.ref[...], th[:, cols]))
        th[0:count, cols] = high.astype(BF16)
        tl[0:count, cols] = low.astype(BF16)
    part = got[0][...].astype(F32)
    for one in got[1:]:
        part = part + one[...].astype(F32)
    lines = slots.lines(slots.held)
    perm.wait(0)
    kx.wait(0)
    left, right = sparse_factors(slots, count, part, lines, kx.ref, fj_ref)
    moved = dot(th[0:count, :], perm.ref[...]) + dot(tl[0:count, :], perm.ref[...])
    out_ref[...] = (moved + dot(left, right)).astype(BF16)

    k = lax.broadcasted_iota(jnp.int32, (128, cells), 0)
    lane = lax.broadcasted_iota(jnp.int32, (128, cells), 1)
    total = dot(part.astype(BF16), same_cells(lines, lines), NT)
    for t in range(slots.slots):
        layer, row, column = slots.held(jnp.int32(t))
        first = pl.multiple_of(over(row, 16) * 16, 16)
        tile = x.ref[:, layer, pl.ds(first, 16), :].astype(F32)
        inside = lax.broadcasted_iota(jnp.int32, (1, 16, 128), 1) == row - first
        line = jnp.sum(jnp.where(inside, tile, 0.0), axis=1).astype(BF16)
        at = lane - t * BRICK
        hot = (k == column + at) & (at >= 0) & (at < BRICK)
        total = total + dot(line, jnp.where(hot, 1.0, 0.0).astype(BF16))
    spread_groups(slots.me, total.astype(BF16).astype(F32), lats)


def basis_kernel(rows_ref, kx_ref, ix_ref, fj_ref, bt):
    bt_ref = bt.ref
    rows, cells = bt_ref.shape
    width = 256
    piece = min(rows, 256)

    def place(i, carry):
        at = pl.ds(pl.multiple_of(i * width, width), width)
        lines = rows_ref[:, at]
        iota = lax.broadcasted_iota(jnp.int32, (128, width), 0).astype(F32)

        def hot(r):
            one = jnp.where(iota == lines[r : r + 1, :], 1.0, 0.0).astype(BF16)
            return jnp.concatenate([one, one], axis=0)

        tj = dot(fj_ref[...], hot(1))[0:1, :]
        hi, hk = hot(0), hot(2)
        for r in range(rows // piece):
            rs = slice(r * piece, (r + 1) * piece)
            value = dot(kx_ref[rs, :], hk) * (dot(ix_ref[rs, :], hi) * tj)
            bt_ref[rs, at] = value.astype(BF16)
        bt.start(i)
        return carry

    lax.fori_loop(0, cells // width, place, 0)


def send_cells(modes_rows, scale_row, bt, sy_ref, turned):
    bt_ref = bt.ref
    devices2, chan, cells = sy_ref.shape
    value = jnp.transpose(modes_rows)[0 : 2 * chan, :] * scale_row
    high, low = split(value)
    turned[...] = jnp.concatenate([high, low], axis=0).astype(BF16)
    per = max(1, 256 // cells)
    width = per * cells

    def step(i, carry):
        at = pl.ds(pl.multiple_of(i * width, width), width)
        o = dot(turned[...], bt_ref[:, at])
        o = (o[0 : 2 * chan] + o[2 * chan :]).astype(BF16)
        for j in range(per):
            for c in range(2):
                sy_ref[(i * per + j) * 2 + c] = o[
                    c * chan : (c + 1) * chan, j * cells : (j + 1) * cells
                ]
        return carry

    lax.fori_loop(0, devices2 // 2 // per, step, 0, unroll=2)


def block_mask():
    lane = over(lax.broadcasted_iota(jnp.int32, (8, 512), 1), 64)
    return jnp.where(lane == lax.broadcasted_iota(jnp.int32, (8, 512), 0), 1.0, 0.0)


def start_weights(core, w_ref, buffer, sems):
    own = buffer.shape[0]
    pieces = sems.shape[0]
    size = own // pieces
    copies = []
    for i in range(pieces):
        source = w_ref.at[pl.ds(core[0] * own + i * size, size)]
        copies.append(pltpu.make_async_copy(source, buffer.at[pl.ds(i * size, size)], sems.at[i]))
        copies[-1].start()
    return copies


def mix_kernel(
    core, recv_ref, fi_ref, scale_ref, w, bt,
    sy_ref, coef_ref, coef, mix, turned, w_ref, sems,
):
    copies = start_weights(core, w, w_ref, sems)
    number = coef.shape[0] // MODES
    chan = coef_ref.shape[0] // 2
    coef[...] = jnp.zeros_like(coef)
    mix[...] = jnp.zeros_like(mix)
    for c in range(2):
        if len(recv_ref.shape) == 4:
            got = recv_ref[:, c].astype(F32)
            got = got.reshape(got.shape[0] * got.shape[1], got.shape[2]).astype(BF16)
        else:
            got = recv_ref[c]
        x = dot(fi_ref[...], got)
        x = x[0:MODES] + x[MODES:]
        for n in range(number):
            coef[n * MODES : (n + 1) * MODES, c * chan : (c + 1) * chan] = x[
                :, n * chan : (n + 1) * chan
            ]
    coef_ref[...] = jnp.transpose(coef[...])[0 : 2 * chan, :]
    mask = block_mask()

    def one(n, carry):
        for group in range(MODES // 8):
            rows = pl.ds(pl.multiple_of(n * MODES + group * 8, 8), 8)
            c8 = coef[rows, :]
            c128 = c8 + pltpu.roll(c8, 64, 1)
            high, low = split(jnp.concatenate([c128] * 4, axis=1) * mask)
            left = jnp.concatenate([high, low], axis=0).astype(BF16)
            o = dot(left, w_ref[n, group * 8 : (group + 1) * 8].reshape(512, 64))
            mix[rows, 0:64] = o[0:8] + o[8:16]
        return carry

    for part, copy in enumerate(copies):
        copy.wait()
        each = number // len(copies)
        lax.fori_loop(part * each, (part + 1) * each, one, 0, unroll=4)
    bt.wait(0)
    send_cells(mix[...], scale_ref[...], bt, sy_ref, turned)


def mixback_kernel(
    core, recv_ref, column_ref, scale_ref, w, bt,
    sy_ref, gm_ref, gm, mix, turned, w_ref, sems, g_ref,
):
    bt_ref = bt.ref
    copies = start_weights(core, w, w_ref, sems)
    devices2, chan, cells = recv_ref.shape
    number = gm.shape[0] // MODES
    gm[...] = jnp.zeros_like(gm)

    def place(i, carry):
        at = pl.ds(pl.multiple_of(i * cells, cells), cells)
        for c in range(2):
            g_ref[c * chan : (c + 1) * chan, at] = recv_ref[2 * i + c]
        return carry

    lax.fori_loop(0, devices2 // 2, place, 0)
    bt.wait(0)
    gm[:, 0:64] = dot(bt_ref[...], g_ref[...], NT) * column_ref[...]
    gm_ref[...] = jnp.transpose(gm[...])[0:64, :]
    mask = block_mask()

    def one(n, carry):
        for group in range(MODES // 8):
            rows = pl.ds(pl.multiple_of(n * MODES + group * 8, 8), 8)
            high, low = split(gm[rows, 0:64])
            left = jnp.concatenate([high, low], axis=0).astype(BF16)
            o = dot(left, w_ref[n, group * 8 : (group + 1) * 8].reshape(512, 64), NT)
            o = (o[0:8] + o[8:16]) * mask
            o = (o[:, 0:128] + o[:, 128:256]) + (o[:, 256:384] + o[:, 384:512])
            mix[rows, :] = o + pltpu.roll(o, 64, 1)
        return carry

    for part, copy in enumerate(copies):
        copy.wait()
        each = number // len(copies)
        lax.fori_loop(part * each, (part + 1) * each, one, 0, unroll=2)
    send_cells(mix[...], scale_ref[...], bt, sy_ref, turned)


def point_kernel(subs, recv_ref, rg_ref, *rest):
    lats, (g_ref, b_ref) = rest[:subs], rest[subs:]
    preact = jnp.sum(recv_ref[...].astype(F32), axis=0)
    for one in lats:
        preact = preact + one[...].astype(F32)
    value, slope = gelu_pair(preact)
    b_ref[...] = value.astype(BF16).astype(F32)
    g = (slope * rg_ref[...]).astype(BF16)

    def copy(i, carry):
        g_ref[i] = g
        return carry

    lax.fori_loop(0, g_ref.shape[0], copy, 0)


def own_kernel(make, s0, s1, s2, s3, rows_ref, recv_ref, out_ref):
    slots = make((s0, s1, s2, s3))
    cells = out_ref.shape[1]
    mine = slots.lines(slots.own)
    total = jnp.zeros(out_ref.shape, F32)
    for u in range(slots.subs):
        source = slots.slab * slots.subs + u
        lines = rows_ref[:, pl.ds(pl.multiple_of(source * cells, cells), cells)]
        same = same_cells(mine, [lines[d : d + 1, :] for d in range(3)])
        total = total + dot(recv_ref[source * 2 + slots.core], same, NT)
    out_ref[...] = total


def outer_kernel(place, coef_ref, grad_ref, *rest):
    out_ref, left = rest[-2:]
    coef = coef_ref[...]
    grad = jnp.transpose(grad_ref[...])
    chan = coef.shape[0]
    lane = lax.broadcasted_iota(jnp.int32, (1, 256), 1)
    row = lax.broadcasted_iota(jnp.int32, (256, 256), 0)
    column = lax.broadcasted_iota(jnp.int32, (256, 256), 1)
    picked = modulo(row, 4) == over(column, 64)
    for chunk in range(coef.shape[1] // 64):
        part = coef[:, chunk * 64 : (chunk + 1) * 64]
        high, low = split(part)
        wide = jnp.concatenate([high, low, high, jnp.zeros_like(high)], axis=1)
        for x in range(16):
            left[x * chan : (x + 1) * chan, :] = jnp.where(
                over(modulo(lane, 64), 4) == x, wide, 0.0
            ).astype(BF16)
        g = grad[chunk * 64 : (chunk + 1) * 64, :]
        high, low = split(g)
        tall = jnp.concatenate([high, high, low, jnp.zeros_like(high)], axis=0)
        two = jnp.concatenate([tall, tall], axis=1)
        right = jnp.where(picked, jnp.concatenate([two, two], axis=1), 0.0).astype(BF16)
        o = dot(left[...], right).astype(BF16)
        for x in range(64):
            at = chunk * 64 + x
            out_ref[at // MODES, at % MODES] = o[
                (x // 4) * chan : (x // 4 + 1) * chan, (x % 4) * 64 : (x % 4 + 1) * 64
            ]


def tables(chan, planes, devices, count_j, count_k):
    count_i = planes * devices
    raw_i, norm_i = raw_basis(count_i)
    raw_j, norm_j = raw_basis(count_j)
    raw_k, norm_k = raw_basis(count_k)
    fk_high, fk_low = halves(raw_k * norm_k)
    fk = np.zeros((4, count_k, 2, 4, MODES), jnp.bfloat16)
    for c in range(4):
        fk[c, :, 0, c] = fk_high
        fk[c, :, 1, c] = fk_low
    fj_high, fj_low = halves(raw_j * norm_j)
    left = np.zeros((2, MODES, planes, planes, count_j), jnp.bfloat16)
    for p in range(planes):
        left[0, :, p, p] = fj_high.T
        left[1, :, p, p] = fj_low.T
    left = left.reshape(2, MODES * planes, planes * count_j)
    fi_high, fi_low = halves(raw_i * norm_i)
    fi = np.concatenate([fi_high.T, fi_low.T], axis=0)

    def expand(raw, order):
        high, low = halves(raw)
        both = np.concatenate([high.T, low.T], axis=1)
        return np.repeat(both, MODES, axis=0) if order == "rep" else np.tile(both, (MODES, 1))

    both = np.concatenate(halves(raw_k * norm_k), axis=0)
    kc = np.repeat(both, chan, axis=1)
    fj_both = np.concatenate([fj_high.T, fj_low.T], axis=1)
    fjp = np.repeat(fj_both, planes, axis=0)
    kx = expand(raw_k, "rep")
    ix = expand(raw_i, "tile")
    fj_rows = np.concatenate([h.T for h in halves(raw_j)], axis=1)
    norm_nl = np.repeat(norm_k, MODES) * np.tile(norm_i, MODES)
    return {
        "fk": fk.reshape(4 * count_k, 8 * MODES),
        "lh": left[0],
        "ll": left[1],
        "fi": fi,
        "kc": kc,
        "fjp": fjp,
        "kx": kx,
        "ix": ix,
        "fj": fj_rows,
        "norm_nl": norm_nl.astype(np.float32),
        "norm_j": norm_j.astype(np.float32),
    }


def permutation(chan):
    perm = np.zeros((chan, MODES, MODES, chan), jnp.bfloat16)
    for c in range(chan):
        for n in range(MODES):
            perm[c, n, n, c] = 1
    return perm.reshape(chan * MODES, MODES * chan)


def body(
    coords,
    features,
    valid_count,
    pair_block,
    pair_brick,
    pair_count,
    geometry,
    encoder_first,
    encoder_bias,
    encoder_second,
    decoder_first,
    decoder_bias,
    decoder_second,
    spectral,
    cotangent,
):
    subs = lax.axis_size("sub")
    devices = lax.axis_size("slab") * subs
    every = ("slab", "sub", "chan")
    slab_index = lax.axis_index("slab")
    sub_index = lax.axis_index("sub")
    chan_index = lax.axis_index("chan")
    pair = slab_index * subs + sub_index
    blocks_here = valid_count.shape[0]
    chan, planes, count_j, count_k = geometry.shape
    points = features.shape[0]
    hidden = encoder_first.shape[1]
    slots = subs * CAP
    cells = slots * BRICK
    all_cells = devices * cells
    own = spectral.shape[0] // 2
    rows = own * MODES
    split_n = MODES // own
    tab = {k: v if k.startswith("norm") else jnp.asarray(v) for k, v in
           tables(chan, planes, devices, count_j, count_k).items()}
    per_row = count_k // BRICK

    def place(values):
        return values // (count_j * per_row), values // per_row % count_j, values % per_row

    def make(refs):
        return Slots(refs, subs, planes, count_j, per_row)

    def shape(dims, kind=F32):
        return jax.ShapeDtypeStruct(dims, kind)

    def hold(*values):
        return lax.optimization_barrier(values)

    def ring(values, axis, size):
        moved = [values[0]]
        for k in range(1, size):
            moved.append(lax.ppermute(values[k], axis, [(i, (i + k) % size) for i in range(size)]))
        return moved

    scal = [(v, "scalar") for v in (pair_block, pair_brick, pair_count, valid_count)]
    features_t, cotangent_t = features.T, cotangent.T
    enc_layers = [encoder_first, encoder_bias[None], encoder_second.T]
    dec_layers = [decoder_first, decoder_bias[None], decoder_second.T]
    wide = BRICK * hidden
    by_slot = (max(1, slots // 4), 0)
    whole = "whole"
    w1_scratch = pltpu.VMEM((4, hidden, BLOCK), F32)
    hidden_shape = shape((slots * wide, BLOCK), BF16)
    values_shape = shape((chan, cells), BF16)

    def wholes(*arrays):
        return [(a, whole) for a in arrays]

    def net(sign, weight, keep, f, layers):
        outs = [(shape((slots * chan, wide), BF16), by_slot)]
        if keep:
            outs += [(hidden_shape, by_slot)] * 2 + [(shape((chan, cells)), whole)]
        else:
            outs += [(values_shape, whole)] * subs
        return call(
            functools.partial(net_kernel, sign, weight, keep, make),
            [*scal, *wholes(coords, f, *layers)], outs, [w1_scratch, pltpu.VMEM((wide, 128), BF16)],
        )

    with jax.named_scope("encoder_points"):
        enc_g, *message = net(1.0, QUADRATURE, False, features_t, enc_layers)
    with jax.named_scope("partial_exchange"):
        partials = ring(message, "sub", subs)

    slabs = devices // subs
    with jax.named_scope("slots_all"):
        pair_brick, _ = hold(pair_brick, message[0])
        around = jnp.stack(ring([pair_brick[0]] * slabs, "slab", slabs))
        bricks_all = jnp.take(around, (slab_index - jnp.arange(slabs)) % slabs, axis=0)
    lanes = chan * MODES
    with jax.named_scope("dense_transform"):
        dense, *latents = call(
            functools.partial(dense_kernel, subs, make),
            [*scal, *wholes(tab["fk"], tab["fjp"], *partials), (geometry, (planes, 1)),
             (tab["lh"], (1, 0)), (tab["ll"], (1, 0)), (jnp.asarray(permutation(chan)), (1, 0)),
             (tab["kc"], (1, 0))],
            [(shape((MODES * planes, lanes), BF16), whole), *[(values_shape, whole)] * subs],
            [pltpu.VMEM((planes * count_j, lanes), BF16)] * 2, 8e9, 1e7,
        )
    with jax.named_scope("dense_exchange"):
        dense = dense.reshape(MODES, planes, split_n, own * chan)
        dense = dense.transpose(0, 2, 1, 3).reshape(MODES * split_n, planes, own * chan)
        dense, pair = hold(dense, pair)
        dense = lax.all_to_all(dense, every, 0, 0, tiled=True)
        dense = dense.reshape(devices, 2, planes, own * chan)
        if planes % 8:
            dense = dense.transpose(1, 0, 2, 3).reshape(2, devices * planes, own * chan)
    with jax.named_scope("latent_exchange"):
        latents = ring(latents, "sub", subs)

    first_pair = (pair * 2 + chan_index) * own
    mode_j = first_pair // MODES
    kx = tab["kx"]
    norm_nl = jnp.asarray(tab["norm_nl"])
    if split_n > 1:
        begin = first_pair % MODES * MODES
        kx = lax.dynamic_slice_in_dim(kx, begin, rows, 0)
        norm_nl = lax.dynamic_slice_in_dim(norm_nl, begin, rows, 0)
    scale = norm_nl * lax.dynamic_index_in_dim(jnp.asarray(tab["norm_j"]), mode_j, 0, keepdims=False)
    scale_column, scale_row = scale[:, None], scale[None, :]
    fj = lax.dynamic_slice_in_dim(tab["fj"], mode_j, 1, 0)
    fj = jnp.broadcast_to(fj, (16, fj.shape[1]))
    layer, row, column = place(bricks_all)
    slab_of = jnp.arange(slabs, dtype=jnp.int32)[:, None, None, None]
    owner = jnp.arange(subs, dtype=jnp.int32)[None, None, :, None]
    plane = (slab_of * subs + owner) * planes + layer
    lines = jnp.stack([plane.reshape(-1), row.reshape(-1), column.reshape(-1) * BRICK])
    lines = jnp.repeat(lines, BRICK, axis=1)
    inner = jnp.arange(all_cells, dtype=jnp.int32) % BRICK
    rows_all = (lines + jnp.stack([0 * inner, 0 * inner, inner])).astype(F32)

    with jax.named_scope("cell_basis"):
        (bt,) = call(
            basis_kernel,
            wholes(rows_all, kx, tab["ix"][:rows], fj),
            [(shape((rows, all_cells), BF16), (all_cells // 256, 1))], [], 5e9, 8e6,
        )

    readers = shape((2 * devices, chan, cells), BF16)
    by_mode = shape((2 * chan, rows))
    mode_scratch = [
        pltpu.VMEM((rows, 128), F32),
        pltpu.VMEM((rows, 128), F32),
        pltpu.VMEM((4 * chan, rows), BF16),
        pltpu.VMEM((own, MODES, 2 * chan, 2 * chan), BF16),
        pltpu.SemaphoreType.DMA((min(8, own),)),
    ]
    core = chan_index.astype(jnp.int32).reshape(1)
    with jax.named_scope("mix"):
        bt, *latents = hold(bt, *latents)
        sent, coefficient = call(
            mix_kernel,
            [(core, "scalar"), *wholes(dense, tab["fi"], scale_row), (spectral, "raw"), (bt, (1, 0))],
            [(readers, whole), (by_mode, whole)], mode_scratch, 4e9, 2e7,
        )
    with jax.named_scope("preact_exchange"):
        arrived = lax.all_to_all(sent, every, 0, 0, tiled=True)
    swap = [(0, 1), (1, 0)]
    with jax.named_scope("coefficient_swap"):
        coef_near = lax.dynamic_slice_in_dim(coefficient, chan_index * chan, chan, 0)
        coef_sent = lax.dynamic_slice_in_dim(coefficient, (1 - chan_index) * chan, chan, 0)
        coef_far = lax.ppermute(coef_sent, "chan", swap)

    with jax.named_scope("decoder_points"):
        cotangent_t, _ = hold(cotangent_t, sent)
        dec_g, dec_slope, dec_hid, read_grads = net(
            -1.0, 1.0 / BRICK, True, cotangent_t, dec_layers
        )

    with jax.named_scope("cell_values"):
        arrived, read_grads, coef_far = hold(arrived, read_grads, coef_far)
        cell_grads, bricks = call(
            functools.partial(point_kernel, subs),
            wholes(arrived, read_grads, *latents),
            [(readers, whole), (shape((chan, cells)), whole)], [], 1e6, 1e6,
        )
    with jax.named_scope("cell_grads_all"):
        all_grads = lax.all_to_all(cell_grads, every, 0, 0, tiled=True)

    def back(sign, weight, decode, f, layers, operands, saved):
        outs = [(shape((chan + 8, hidden)), whole)]
        scratch = []
        if decode:
            outs.append((shape((chan, points), BF16), whole))
            scratch.append(pltpu.VMEM((blocks_here, chan, BLOCK), F32))
        return call(
            functools.partial(back_kernel, sign, weight, decode, make),
            [*scal, *wholes(coords, f, layers[2], *operands),
             *[(v, by_slot) for v in saved]],
            outs, scratch,
        )

    with jax.named_scope("decoder_back"):
        dec_grads, decoded = back(
            -1.0, 1.0 / BRICK, True, cotangent_t, dec_layers, [bricks],
            [dec_g, dec_slope, dec_hid],
        )

    with jax.named_scope("encoder_slope"):
        slope_coords, _ = hold(coords, cell_grads)
        (enc_slope,) = call(
            functools.partial(slope_kernel, 1.0, make),
            [*scal, *wholes(slope_coords, *enc_layers[0:2])],
            [(hidden_shape, by_slot)], [w1_scratch], 1e9, 4e6,
        )
    with jax.named_scope("mix_back"):
        all_grads, decoded, enc_slope = hold(all_grads, decoded, enc_slope)
        sent_back, grad_modes = call(
            mixback_kernel,
            [(core, "scalar"), *wholes(all_grads, scale_column, scale_row), (spectral, "raw"),
             (bt, (1, 0))],
            [(readers, whole), (by_mode, whole)],
            mode_scratch + [pltpu.VMEM((2 * chan, all_cells), BF16)], 4e9, 2e7,
        )
    with jax.named_scope("latent_grad_exchange"):
        arrived_back = lax.all_to_all(sent_back, every, 0, 0, tiled=True)
    with jax.named_scope("grad_swap"):
        grad_far = lax.ppermute(grad_modes, "chan", swap)
    with jax.named_scope("own_cells"):
        (own_grads,) = call(
            functools.partial(own_kernel, make),
            [*scal, *wholes(rows_all, all_grads)],
            [(shape((chan, cells)), whole)], [], 1e8, 1e6,
        )

    with jax.named_scope("grad_spectral"):
        block_n = min(8, own)
        steps = own // block_n
        width = block_n * MODES

        def lanes_spec(height):
            return pl.BlockSpec((height, width), lambda n, place: (0, n))

        def outer(half, coef, grad, held):
            more = [] if held is None else [held]
            return pl.pallas_call(
                outer_kernel,
                grid_spec=pltpu.PrefetchScalarGridSpec(
                    num_scalar_prefetch=1,
                    grid=(steps,),
                    in_specs=[lanes_spec(chan), lanes_spec(2 * chan)]
                    + [pl.BlockSpec(memory_space=pl.ANY)] * len(more),
                    out_specs=pl.BlockSpec(
                        (block_n, MODES, chan, 2 * chan),
                        lambda n, place: (place[0] * steps + n, 0, 0, 0),
                    ),
                    scratch_shapes=[pltpu.VMEM((16 * chan, 256), BF16)],
                ),
                out_shape=shape((2 * own, MODES, chan, 2 * chan), BF16),
                input_output_aliases={3: 0} if more else {},
                compiler_params=pltpu.CompilerParams(vmem_limit_bytes=VMEM_LIMIT),
                cost_estimate=pl.CostEstimate(
                    flops=10**7, bytes_accessed=10**7, transcendentals=0
                ),
            )(half, coef, grad, *more)

        grad_spectral = outer(core, coef_near, grad_modes, None)

    with jax.named_scope("encoder_back"):
        arrived_back, own_grads, grad_spectral = hold(arrived_back, own_grads, grad_spectral)
        (enc_grads,) = back(
            1.0, QUADRATURE, False, features_t, enc_layers, [own_grads, arrived_back],
            [enc_g, enc_slope],
        )
    with jax.named_scope("grad_spectral_far"):
        grad_far, _ = hold(grad_far, enc_grads)
        grad_spectral = outer(1 - core, coef_far, grad_far, grad_spectral)
    with jax.named_scope("weight_sums"):
        both = jnp.concatenate([enc_grads, dec_grads], axis=1).astype(BF16)
        spread = jnp.broadcast_to(both[None], (devices,) + both.shape)
        total = jnp.sum(
            lax.all_to_all(spread, ("slab", "sub"), 0, 0, tiled=True).astype(F32), axis=0
        )
        small = total[chan:]
        small = small + lax.ppermute(small, "chan", swap)
    enc_second = total[:chan, :hidden].T
    dec_second = total[:chan, hidden:].T
    return (
        decoded.T,
        small[0:3, :hidden],
        small[3, :hidden],
        enc_second,
        small[0:3, hidden:],
        small[3, hidden:],
        dec_second,
        grad_spectral,
    )


def solution(mesh):
    placed = (
        P(None, ("groups", "slab", "sub")),
        P(("groups", "slab", "sub"), "chan"),
        P(("groups", "slab", "sub")),
        P(("groups", "slab"), None, None, None),
        P(("groups", "slab"), None, None, None),
        P(("groups", "slab"), None, None),
        P("chan", ("groups", "slab", "sub"), None, None),
        P(),
        P(),
        P(None, "chan"),
        P(),
        P(),
        P(None, "chan"),
        P(("slab", "sub"), None, None, None),
        P(("groups", "slab", "sub"), "chan"),
    )
    return jax.shard_map(
        body,
        mesh=mesh,
        in_specs=placed,
        out_specs=(
            P(("groups", "slab", "sub"), "chan"),
            P("groups", None),
            P("groups"),
            P("groups", "chan"),
            P("groups", None),
            P("groups"),
            P("groups", "chan"),
            P(("groups", "slab", "sub"), None, "chan", None),
        ),
        check_vma=False,
    )
```

```python
import functools

import jax
import jax.numpy as jnp
import numpy as np
from jax import lax
from jax.experimental import pallas as pl
from jax.experimental.pallas import tpu as pltpu
from jax.sharding import PartitionSpec as P

MODES = 32
BLOCK = 128
BRICK = 8
CAP = 4
RADIUS = 4.0
QUADRATURE = 0.0625

F32 = jnp.float32
BF16 = jnp.bfloat16
MIB = 1 << 20

NN = (((1,), (0,)), ((), ()))
NT = (((1,), (1,)), ((), ()))
TN = (((0,), (0,)), ((), ()))


def dot(a, b, dims=NN):
    return lax.dot_general(a, b, dims, preferred_element_type=F32)


def raw_basis(length):
    half = MODES // 2
    n = np.arange(length)[:, None]
    m = np.arange(half)[None, :]
    values = np.concatenate(
        [np.cos(2 * np.pi * m * n / length), np.sin(2 * np.pi * (m + 1) * n / length)], axis=1
    )
    norm = np.full(MODES, np.sqrt(2.0 / length))
    norm[0] = np.sqrt(1.0 / length)
    return values, norm


def halves(values):
    high = np.asarray(values, np.float32).astype(jnp.bfloat16)
    low = (np.asarray(values, np.float64) - high.astype(np.float64)).astype(jnp.bfloat16)
    return high, low


def split(value):
    high = value.astype(BF16).astype(F32)
    return high, value - high


def over(x, d):
    return x >> (d.bit_length() - 1) if d & (d - 1) == 0 else lax.div(x, d)


def modulo(x, d):
    return x & (d - 1) if d & (d - 1) == 0 else lax.rem(x, d)


def gelu_pair(x):
    a = 0.7978845608028654
    b = a * 0.044715
    x2 = x * x
    t = jnp.tanh(x * (a + b * x2))
    half = 0.5 + 0.5 * t
    slope = half + (0.5 * x) * (1.0 - t * t) * (a + (3.0 * b) * x2)
    return x * half, slope


VMEM_LIMIT = 62 * MIB


class Late:
    def __init__(self, source, target, sems, pieces, axis, held, ahead):
        self.source, self.target, self.sems, self.ahead = source, target, sems, ahead
        self.pieces, self.axis, self.ref = pieces, axis, held

    def copy(self, i):
        size = self.ref.shape[self.axis] // self.pieces
        if isinstance(i, int):
            piece = pl.ds(i * size, size)
        else:
            piece = pl.ds(pl.multiple_of(i * size, size), size)
        at = (slice(None),) * self.axis + (piece,)
        return pltpu.make_async_copy(self.source.at[at], self.target.at[at], self.sems.at[i])

    def start(self, i):
        self.copy(i).start()

    def wait(self, i):
        self.copy(i).wait()


def call(kernel, ins, outs, scratch=(), flops=1e9, nbytes=8e6):
    buffers, sems = [], []
    modes_in, modes_out = [m for _, m in ins], [m for _, m in outs]
    for array, mode in [*ins, *outs]:
        if mode == "raw":
            continue
        space = pltpu.SMEM if mode == "scalar" else pltpu.VMEM
        buffers.append(space(array.shape, array.dtype))
        sems.append(pltpu.SemaphoreType.DMA((mode[0] if isinstance(mode, tuple) else 1,)))

    def wrapped(*refs):
        arrays = refs[: len(ins) + len(outs)]
        rest = refs[len(ins) + len(outs) :]
        held, signals = rest[: len(buffers)], rest[len(buffers) : 2 * len(buffers)]
        more = rest[2 * len(buffers) :]
        objects, early, late, place = [], [], [], 0
        for i, (array, mode) in enumerate(zip(arrays, modes_in + modes_out)):
            if mode == "raw":
                objects.append(array)
                continue
            buffer, sem = held[place], signals[place]
            place += 1
            pieces, axis = mode if isinstance(mode, tuple) else (1, 0)
            source, target = (array, buffer) if i < len(ins) else (buffer, array)
            one = Late(source, target, sem, pieces, axis, buffer, i < len(ins))
            if isinstance(mode, tuple):
                objects.append(one)
                late.append((i, one))
            else:
                objects.append(buffer)
                early.append((i, pltpu.make_async_copy(source, target, sem.at[0])))
        for i, one in early:
            if i < len(ins):
                one.start()
        for i, one in late:
            if i < len(ins):
                for j in range(one.pieces):
                    one.start(j)
        for i, one in early:
            if i < len(ins):
                one.wait()
        kernel(*objects, *more)
        for i, one in early:
            if i >= len(ins):
                one.start()
        for i, one in early:
            if i >= len(ins):
                one.wait()
        for i, one in late:
            if i >= len(ins):
                for j in range(one.pieces):
                    one.wait(j)

    hbm = pl.BlockSpec(memory_space=pl.ANY)
    return pl.pallas_call(
        wrapped,
        out_shape=[jax.ShapeDtypeStruct(o.shape, o.dtype) for o, _ in outs],
        in_specs=[hbm] * len(ins),
        out_specs=[hbm] * len(outs),
        scratch_shapes=[*buffers, *sems, *scratch],
        compiler_params=pltpu.CompilerParams(vmem_limit_bytes=VMEM_LIMIT),
        cost_estimate=pl.CostEstimate(
            flops=int(flops), bytes_accessed=int(nbytes), transcendentals=0
        ),
    )(*[a for a, _ in ins])


class Slots:
    def __init__(self, refs, subs, planes, count_j, per_row):
        self.block_ref, self.brick_ref, self.count_ref, self.valid_ref = refs
        self.subs, self.planes = subs, planes
        self.count_j, self.per_row = count_j, per_row
        self.slots = subs * CAP
        self.slab = lax.axis_index("slab")
        self.me = lax.axis_index("sub")
        self.core = lax.axis_index("chan")

    def block(self, s):
        return self.block_ref[0, self.me, over(s, CAP), modulo(s, CAP)]

    def place(self, brick):
        row = modulo(over(brick, self.per_row), self.count_j)
        column = modulo(brick, self.per_row) * BRICK
        return over(brick, self.count_j * self.per_row), row, column

    def own(self, s):
        layer, row, column = self.place(self.brick_ref[0, self.me, over(s, CAP), modulo(s, CAP)])
        first = (self.slab * self.subs + over(s, CAP)) * self.planes
        return first + layer, row, column

    def held(self, t):
        return self.place(self.brick_ref[0, over(t, CAP), self.me, modulo(t, CAP)])

    def live(self, s):
        count = self.count_ref[0, self.me, over(s, CAP)]
        return jnp.where(modulo(s, CAP) < count, 1.0, 0.0)

    def valid(self, b):
        return self.valid_ref[b]

    def lines(self, which):
        cells = self.slots * BRICK
        lane = lax.broadcasted_iota(jnp.int32, (1, cells), 1)
        rows = [jnp.zeros((1, cells), jnp.int32)] * 3
        for s in range(self.slots):
            here = over(lane, BRICK) == s
            values = which(jnp.int32(s))
            rows = [jnp.where(here, v, r) for v, r in zip(values, rows)]
        rows[2] = rows[2] + modulo(lane, BRICK)
        return [r.astype(F32) for r in rows]


def cell_number(lines):
    return lines[0] * 16384.0 + lines[1] * 128.0 + lines[2]


def same_cells(column_lines, lines):
    number = cell_number(column_lines)
    tall = jnp.transpose(jnp.broadcast_to(number, (number.shape[1], number.shape[1])))
    return jnp.where(tall[:, 0:1] == cell_number(lines), 1.0, 0.0).astype(BF16)


def columns(first, bias, w1):
    hidden = first.shape[1]
    rows = jnp.concatenate(
        [first[...] * (1.0 / RADIUS), bias[...], jnp.zeros((124, hidden), F32)], axis=0
    )
    turned = jnp.transpose(rows)
    for d in range(4):
        w1[d] = jnp.broadcast_to(turned[:, d : d + 1], (hidden, BLOCK))


def second_layer(ref):
    return jnp.concatenate([ref[...], ref[...]], axis=1)


def slot_points(slots, s, x_ref):
    at = pl.multiple_of(slots.block(s) * BLOCK, BLOCK)
    xs = x_ref[:, pl.ds(at, BLOCK)]
    place = slots.own(s)
    return at, [(place[d].astype(F32) + 0.5) - xs[d : d + 1, :] for d in range(3)]


def slot_mask(slots, s, weight):
    lanes = lax.broadcasted_iota(jnp.int32, (1, BLOCK), 1)
    return jnp.where(lanes < slots.valid(slots.block(s)), weight, 0.0) * slots.live(s)


def slot_source(slots, s, at, f_ref, weight):
    return (f_ref[:, pl.ds(at, BLOCK)].astype(F32) * slot_mask(slots, s, weight)).astype(BF16)


def first_base(sign, e, w1):
    return w1[3] + sign * (w1[0] * e[0] + w1[1] * e[1] + w1[2] * e[2])


def spread_groups(me, values, outs):
    groups = len(outs)
    cells = values.shape[1]
    width = cells // groups
    lane = over(lax.broadcasted_iota(jnp.int32, (1, cells), 1), width)
    for k in range(groups):
        moved = pltpu.roll(values, (groups - k) % groups * width, 1) if k else values
        outs[k][...] = jnp.where(lane == me, moved, 0.0).astype(BF16)


def loop(slots, step, first, *arrays):
    each = slots // arrays[0].pieces

    def piece(i, carry):
        for array in arrays:
            if array.ahead:
                array.wait(i)
        for j in range(each):
            carry = step(i * each + j, carry)
        for array in arrays:
            if not array.ahead:
                array.start(i)
        return carry

    return lax.fori_loop(0, arrays[0].pieces, piece, first)


def net_kernel(sign, weight, keep, make, s0, s1, s2, s3, x_ref, f_ref, first, bias, second, *rest):
    slots = make((s0, s1, s2, s3))
    if keep:
        g, slope, hid, part_ref, w1, group = rest
    else:
        g, slope, outs, (w1, group) = rest[0], rest[1], rest[2:-2], rest[-2:]
    chan, hidden = second.shape
    wide = BRICK * hidden
    cells = slots.slots * BRICK
    columns(first, bias, w1)
    w2 = jnp.concatenate([second_layer(second)] * (BRICK // 2), axis=1)
    of_row = over(lax.broadcasted_iota(jnp.int32, (wide, 128), 0), hidden)
    at_lane = lax.broadcasted_iota(jnp.int32, (wide, 128), 1)
    group[...] = jnp.where(of_row == at_lane, 1.0, 0.0).astype(BF16)

    def step(s, part):
        at, e = slot_points(slots, s, x_ref)
        f = slot_source(slots, s, at, f_ref, weight)
        base = first_base(sign, e, w1)
        row = pl.multiple_of(s * wide, wide)
        values = []
        for q in range(BRICK):
            value, gradient = gelu_pair(base + (sign * q) * w1[2])
            values.append(value.astype(BF16))
            slope.ref[pl.ds(row + q * hidden, hidden), :] = gradient.astype(BF16)
        all_q = jnp.concatenate(values, axis=0)
        total = dot(f, all_q, NT)
        g.ref[pl.ds(pl.multiple_of(s * chan, chan), chan), :] = total.astype(BF16)
        if keep:
            hid.ref[pl.ds(row, wide), :] = all_q
        high, low = split(total * w2)
        both = jnp.concatenate([high, low], axis=0).astype(BF16)
        sums = dot(both, group[...])
        sums = sums[0:chan] + sums[chan:]
        if cells > 128:
            sums = jnp.concatenate([sums, jnp.zeros((chan, cells - 128), F32)], axis=1)
        return part + pltpu.roll(sums, s * BRICK, 1)

    kept = (g, slope, hid) if keep else (g, slope)
    part = loop(slots.slots, step, jnp.zeros((chan, cells), F32), *kept)
    if keep:
        part_ref[...] = part
    else:
        spread_groups(slots.me, part, outs)


def back_kernel(sign, weight, decode, make, s0, s1, s2, s3, x_ref, f_ref, second, *rest):
    slots = make((s0, s1, s2, s3))
    if decode:
        gp_ref, g, slope, hid, out_ref, dec_ref, dec = rest
        gp = gp_ref[...]
        dec[...] = jnp.zeros_like(dec)
    else:
        own_ref, recv_ref, other_ref, g, slope, out_ref = rest
        gp = own_ref[...] + jnp.sum(recv_ref[...].astype(F32), axis=0)
    chan, hidden = second.shape
    wide = BRICK * hidden
    cells = gp.shape[1]
    w2 = second_layer(second)
    left_half = lax.broadcasted_iota(jnp.int32, (1, 2 * hidden), 1) < hidden

    def step(s, carry):
        acc, grad2 = carry
        at, e = slot_points(slots, s, x_ref)
        f = slot_source(slots, s, at, f_ref, weight)
        row = pl.multiple_of(s * wide, wide)
        gps = pltpu.roll(gp, cells - s * BRICK, 1)
        gs = g.ref[pl.ds(pl.multiple_of(s * chan, chan), chan), :].astype(F32)
        m = []
        for i in range(BRICK // 2):
            both = jnp.where(left_half, gps[:, 2 * i : 2 * i + 1], gps[:, 2 * i + 1 : 2 * i + 2])
            m.append(w2 * both)
            grad2 = grad2 + gs[:, 2 * i * hidden : 2 * (i + 1) * hidden] * both
        m = jnp.concatenate(m, axis=1)
        back = dot(jnp.transpose(m).astype(BF16), f)
        sum0 = jnp.zeros((hidden, BLOCK), F32)
        sum1 = jnp.zeros((hidden, BLOCK), F32)
        for q in range(BRICK):
            value = back[q * hidden : (q + 1) * hidden, :] * slope.ref[
                pl.ds(row + q * hidden, hidden), :
            ].astype(F32)
            sum0 = sum0 + value
            if q:
                sum1 = sum1 + float(q) * value
        scale = sign / RADIUS
        acc = (
            acc[0] + sum0 * (e[0] * scale),
            acc[1] + sum0 * (e[1] * scale),
            acc[2] + (sum0 * (e[2] * scale) + sum1 * scale),
            acc[3] + sum0,
        )
        if decode:
            value = dot(m.astype(BF16), hid.ref[pl.ds(row, wide), :])
            b = slots.block(s)
            dec[b] = dec[b] + value * slot_mask(slots, s, 1.0 / BRICK)
        return acc, grad2

    zero = jnp.zeros((hidden, BLOCK), F32)
    kept = (g, slope, hid) if decode else (g, slope)
    acc, grad2 = loop(
        slots.slots, step, ((zero,) * 4, jnp.zeros((chan, 2 * hidden), F32)), *kept
    )
    sums = [jnp.sum(a, axis=1, keepdims=True) for a in acc]
    packed = jnp.concatenate(sums + [jnp.zeros((hidden, 124), F32)], axis=1)
    second_grad = grad2[:, 0:hidden] + grad2[:, hidden : 2 * hidden]
    grads = jnp.concatenate([second_grad, jnp.transpose(packed)[0:16, :]], axis=0)
    if not decode:
        message = jnp.concatenate([grads, other_ref[...]], axis=1).astype(BF16)

        def copy(i, carry):
            out_ref[i] = message
            return carry

        lax.fori_loop(0, out_ref.shape[0], copy, 0)
    if decode:
        out_ref[...] = grads
        for b in range(dec.shape[0]):
            dec_ref[:, b * BLOCK : (b + 1) * BLOCK] = dec[b].astype(BF16)


def sparse_factors(slots, planes_modes, part, lines, kx_ref, fj_ref):
    chan, cells = part.shape
    lanes = kx_ref.shape[1]
    planes = planes_modes // MODES
    iota = lax.broadcasted_iota(jnp.int32, (128, cells), 0).astype(F32)

    def hot(line):
        one = jnp.where(iota == line, 1.0, 0.0).astype(BF16)
        return jnp.concatenate([one, one], axis=0)

    plane = lax.broadcasted_iota(jnp.int32, (planes_modes, cells), 0)
    here = modulo(plane, planes).astype(F32) == lines[0]
    high, low = split(jnp.where(here, dot(fj_ref[...], hot(lines[1])), 0.0))
    left = jnp.concatenate([high, high, low], axis=1).astype(BF16)
    turned = jnp.transpose(jnp.concatenate([part, jnp.zeros((128 - chan, cells), F32)], axis=0))
    turned = turned[:, 0:chan]
    four = jnp.concatenate([turned] * (128 // chan), axis=1)
    value = dot(hot(lines[2]), kx_ref[...], TN) * jnp.concatenate([four] * (lanes // 128), axis=1)
    high, low = split(value)
    return left, jnp.concatenate([high, low, high], axis=0).astype(BF16)


def dense_kernel(subs, make, s0, s1, s2, s3, fk_ref, fj_ref, *rest):
    got, (x, lh, ll, perm, kx), (out_ref, *lats), (th, tl) = (
        rest[:subs], rest[subs : subs + 5], rest[subs + 5 : -2], rest[-2:]
    )
    slots = make((s0, s1, s2, s3))
    chan, planes, length = x.ref.shape[0:3]
    cells = got[0].shape[1]

    def plane(p, carry):
        rows = pl.ds(pl.multiple_of(p * length, length), length)
        x.wait(p)
        for group in range(chan // 4):
            a = jnp.concatenate([x.ref[4 * group + i, p] for i in range(4)], axis=1)
            t = dot(a, fk_ref[...])
            high, low = split(t[:, 0:128] + t[:, 128:256])
            th[rows, group * 128 : (group + 1) * 128] = high.astype(BF16)
            tl[rows, group * 128 : (group + 1) * 128] = low.astype(BF16)
        return carry

    lax.fori_loop(0, planes, plane, 0)
    lh.wait(0)
    ll.wait(0)
    count = out_ref.shape[0]
    for piece in range(4):
        cols = slice(piece * 256, (piece + 1) * 256)
        r = dot(lh.ref[...], th[:, cols]) + dot(lh.ref[...], tl[:, cols])
        high, low = split(r + dot(ll.ref[...], th[:, cols]))
        th[0:count, cols] = high.astype(BF16)
        tl[0:count, cols] = low.astype(BF16)
    part = got[0][...].astype(F32)
    for one in got[1:]:
        part = part + one[...].astype(F32)
    lines = slots.lines(slots.held)
    perm.wait(0)
    kx.wait(0)
    left, right = sparse_factors(slots, count, part, lines, kx.ref, fj_ref)
    moved = dot(th[0:count, :], perm.ref[...]) + dot(tl[0:count, :], perm.ref[...])
    out_ref[...] = (moved + dot(left, right)).astype(BF16)

    k = lax.broadcasted_iota(jnp.int32, (128, cells), 0)
    lane = lax.broadcasted_iota(jnp.int32, (128, cells), 1)
    total = dot(part.astype(BF16), same_cells(lines, lines), NT)
    for t in range(slots.slots):
        layer, row, column = slots.held(jnp.int32(t))
        first = pl.multiple_of(over(row, 16) * 16, 16)
        tile = x.ref[:, layer, pl.ds(first, 16), :].astype(F32)
        inside = lax.broadcasted_iota(jnp.int32, (1, 16, 128), 1) == row - first
        line = jnp.sum(jnp.where(inside, tile, 0.0), axis=1).astype(BF16)
        at = lane - t * BRICK
        hot = (k == column + at) & (at >= 0) & (at < BRICK)
        total = total + dot(line, jnp.where(hot, 1.0, 0.0).astype(BF16))
    spread_groups(slots.me, total.astype(BF16).astype(F32), lats)


def basis_kernel(rows_ref, kx_ref, ix_ref, fj_ref, bt):
    bt_ref = bt.ref
    rows, cells = bt_ref.shape
    width = 256
    piece = min(rows, 256)

    def place(i, carry):
        at = pl.ds(pl.multiple_of(i * width, width), width)
        lines = rows_ref[:, at]
        iota = lax.broadcasted_iota(jnp.int32, (128, width), 0).astype(F32)

        def hot(r):
            one = jnp.where(iota == lines[r : r + 1, :], 1.0, 0.0).astype(BF16)
            return jnp.concatenate([one, one], axis=0)

        tj = dot(fj_ref[...], hot(1))[0:1, :]
        hi, hk = hot(0), hot(2)
        for r in range(rows // piece):
            rs = slice(r * piece, (r + 1) * piece)
            value = dot(kx_ref[rs, :], hk) * (dot(ix_ref[rs, :], hi) * tj)
            bt_ref[rs, at] = value.astype(BF16)
        bt.start(i)
        return carry

    lax.fori_loop(0, cells // width, place, 0)


def send_cells(modes_rows, scale_row, bt, sy_ref, turned):
    bt_ref = bt.ref
    devices2, chan, cells = sy_ref.shape
    value = jnp.transpose(modes_rows)[0 : 2 * chan, :] * scale_row
    high, low = split(value)
    turned[...] = jnp.concatenate([high, low], axis=0).astype(BF16)
    per = max(1, 256 // cells)
    width = per * cells

    def step(i, carry):
        at = pl.ds(pl.multiple_of(i * width, width), width)
        o = dot(turned[...], bt_ref[:, at])
        o = (o[0 : 2 * chan] + o[2 * chan :]).astype(BF16)
        for j in range(per):
            for c in range(2):
                sy_ref[(i * per + j) * 2 + c] = o[
                    c * chan : (c + 1) * chan, j * cells : (j + 1) * cells
                ]
        return carry

    lax.fori_loop(0, devices2 // 2 // per, step, 0, unroll=2)


def block_mask():
    lane = over(lax.broadcasted_iota(jnp.int32, (8, 512), 1), 64)
    return jnp.where(lane == lax.broadcasted_iota(jnp.int32, (8, 512), 0), 1.0, 0.0)


def start_weights(core, w_ref, buffer, sems):
    own = buffer.shape[0]
    pieces = sems.shape[0]
    size = own // pieces
    copies = []
    for i in range(pieces):
        source = w_ref.at[pl.ds(core[0] * own + i * size, size)]
        copies.append(pltpu.make_async_copy(source, buffer.at[pl.ds(i * size, size)], sems.at[i]))
        copies[-1].start()
    return copies


def mix_kernel(
    core, recv_ref, fi_ref, scale_ref, w, bt,
    sy_ref, coef_ref, coef, mix, turned, w_ref, sems,
):
    copies = start_weights(core, w, w_ref, sems)
    number = coef.shape[0] // MODES
    chan = coef_ref.shape[0] // 2
    coef[...] = jnp.zeros_like(coef)
    mix[...] = jnp.zeros_like(mix)
    for c in range(2):
        if len(recv_ref.shape) == 4:
            got = recv_ref[:, c].astype(F32)
            got = got.reshape(got.shape[0] * got.shape[1], got.shape[2]).astype(BF16)
        else:
            got = recv_ref[c]
        x = dot(fi_ref[...], got)
        x = x[0:MODES] + x[MODES:]
        for n in range(number):
            coef[n * MODES : (n + 1) * MODES, c * chan : (c + 1) * chan] = x[
                :, n * chan : (n + 1) * chan
            ]
    coef_ref[...] = jnp.transpose(coef[...])[0 : 2 * chan, :]
    mask = block_mask()

    def one(n, carry):
        for group in range(MODES // 8):
            rows = pl.ds(pl.multiple_of(n * MODES + group * 8, 8), 8)
            c8 = coef[rows, :]
            c128 = c8 + pltpu.roll(c8, 64, 1)
            high, low = split(jnp.concatenate([c128] * 4, axis=1) * mask)
            left = jnp.concatenate([high, low], axis=0).astype(BF16)
            o = dot(left, w_ref[n, group * 8 : (group + 1) * 8].reshape(512, 64))
            mix[rows, 0:64] = o[0:8] + o[8:16]
        return carry

    for part, copy in enumerate(copies):
        copy.wait()
        each = number // len(copies)
        lax.fori_loop(part * each, (part + 1) * each, one, 0, unroll=4)
    bt.wait(0)
    send_cells(mix[...], scale_ref[...], bt, sy_ref, turned)


def mixback_kernel(
    core, recv_ref, column_ref, scale_ref, w, bt,
    sy_ref, gm_ref, gm, mix, turned, w_ref, sems, g_ref,
):
    bt_ref = bt.ref
    copies = start_weights(core, w, w_ref, sems)
    devices2, chan, cells = recv_ref.shape
    number = gm.shape[0] // MODES
    gm[...] = jnp.zeros_like(gm)

    def place(i, carry):
        at = pl.ds(pl.multiple_of(i * cells, cells), cells)
        for c in range(2):
            g_ref[c * chan : (c + 1) * chan, at] = recv_ref[2 * i + c]
        return carry

    lax.fori_loop(0, devices2 // 2, place, 0)
    bt.wait(0)
    gm[:, 0:64] = dot(bt_ref[...], g_ref[...], NT) * column_ref[...]
    gm_ref[...] = jnp.transpose(gm[...])[0:64, :]
    mask = block_mask()

    def one(n, carry):
        for group in range(MODES // 8):
            rows = pl.ds(pl.multiple_of(n * MODES + group * 8, 8), 8)
            high, low = split(gm[rows, 0:64])
            left = jnp.concatenate([high, low], axis=0).astype(BF16)
            o = dot(left, w_ref[n, group * 8 : (group + 1) * 8].reshape(512, 64), NT)
            o = (o[0:8] + o[8:16]) * mask
            o = (o[:, 0:128] + o[:, 128:256]) + (o[:, 256:384] + o[:, 384:512])
            mix[rows, :] = o + pltpu.roll(o, 64, 1)
        return carry

    for part, copy in enumerate(copies):
        copy.wait()
        each = number // len(copies)
        lax.fori_loop(part * each, (part + 1) * each, one, 0, unroll=2)
    send_cells(mix[...], scale_ref[...], bt, sy_ref, turned)


def point_kernel(subs, recv_ref, rg_ref, *rest):
    lats, (g_ref, b_ref) = rest[:subs], rest[subs:]
    preact = jnp.sum(recv_ref[...].astype(F32), axis=0)
    for one in lats:
        preact = preact + one[...].astype(F32)
    value, slope = gelu_pair(preact)
    b_ref[...] = value.astype(BF16).astype(F32)
    g = (slope * rg_ref[...]).astype(BF16)

    def copy(i, carry):
        g_ref[i] = g
        return carry

    lax.fori_loop(0, g_ref.shape[0], copy, 0)


def own_kernel(make, s0, s1, s2, s3, rows_ref, recv_ref, out_ref):
    slots = make((s0, s1, s2, s3))
    cells = out_ref.shape[1]
    mine = slots.lines(slots.own)
    total = jnp.zeros(out_ref.shape, F32)
    for u in range(slots.subs):
        source = slots.slab * slots.subs + u
        lines = rows_ref[:, pl.ds(pl.multiple_of(source * cells, cells), cells)]
        same = same_cells(mine, [lines[d : d + 1, :] for d in range(3)])
        total = total + dot(recv_ref[source * 2 + slots.core], same, NT)
    out_ref[...] = total


def outer_kernel(place, coef_ref, grad_ref, *rest):
    out_ref, left = rest[-2:]
    coef = coef_ref[...]
    grad = jnp.transpose(grad_ref[...])
    chan = coef.shape[0]
    lane = lax.broadcasted_iota(jnp.int32, (1, 256), 1)
    row = lax.broadcasted_iota(jnp.int32, (256, 256), 0)
    column = lax.broadcasted_iota(jnp.int32, (256, 256), 1)
    picked = modulo(row, 4) == over(column, 64)
    for chunk in range(coef.shape[1] // 64):
        part = coef[:, chunk * 64 : (chunk + 1) * 64]
        high, low = split(part)
        wide = jnp.concatenate([high, low, high, jnp.zeros_like(high)], axis=1)
        for x in range(16):
            left[x * chan : (x + 1) * chan, :] = jnp.where(
                over(modulo(lane, 64), 4) == x, wide, 0.0
            ).astype(BF16)
        g = grad[chunk * 64 : (chunk + 1) * 64, :]
        high, low = split(g)
        tall = jnp.concatenate([high, high, low, jnp.zeros_like(high)], axis=0)
        two = jnp.concatenate([tall, tall], axis=1)
        right = jnp.where(picked, jnp.concatenate([two, two], axis=1), 0.0).astype(BF16)
        o = dot(left[...], right).astype(BF16)
        for x in range(64):
            at = chunk * 64 + x
            out_ref[at // MODES, at % MODES] = o[
                (x // 4) * chan : (x // 4 + 1) * chan, (x % 4) * 64 : (x % 4 + 1) * 64
            ]


def tables(chan, planes, devices, count_j, count_k):
    count_i = planes * devices
    raw_i, norm_i = raw_basis(count_i)
    raw_j, norm_j = raw_basis(count_j)
    raw_k, norm_k = raw_basis(count_k)
    fk_high, fk_low = halves(raw_k * norm_k)
    fk = np.zeros((4, count_k, 2, 4, MODES), jnp.bfloat16)
    for c in range(4):
        fk[c, :, 0, c] = fk_high
        fk[c, :, 1, c] = fk_low
    fj_high, fj_low = halves(raw_j * norm_j)
    left = np.zeros((2, MODES, planes, planes, count_j), jnp.bfloat16)
    for p in range(planes):
        left[0, :, p, p] = fj_high.T
        left[1, :, p, p] = fj_low.T
    left = left.reshape(2, MODES * planes, planes * count_j)
    fi_high, fi_low = halves(raw_i * norm_i)
    fi = np.concatenate([fi_high.T, fi_low.T], axis=0)

    def expand(raw, order):
        high, low = halves(raw)
        both = np.concatenate([high.T, low.T], axis=1)
        return np.repeat(both, MODES, axis=0) if order == "rep" else np.tile(both, (MODES, 1))

    both = np.concatenate(halves(raw_k * norm_k), axis=0)
    kc = np.repeat(both, chan, axis=1)
    fj_both = np.concatenate([fj_high.T, fj_low.T], axis=1)
    fjp = np.repeat(fj_both, planes, axis=0)
    kx = expand(raw_k, "rep")
    ix = expand(raw_i, "tile")
    fj_rows = np.concatenate([h.T for h in halves(raw_j)], axis=1)
    norm_nl = np.repeat(norm_k, MODES) * np.tile(norm_i, MODES)
    return {
        "fk": fk.reshape(4 * count_k, 8 * MODES),
        "lh": left[0],
        "ll": left[1],
        "fi": fi,
        "kc": kc,
        "fjp": fjp,
        "kx": kx,
        "ix": ix,
        "fj": fj_rows,
        "norm_nl": norm_nl.astype(np.float32),
        "norm_j": norm_j.astype(np.float32),
    }


def permutation(chan):
    perm = np.zeros((chan, MODES, MODES, chan), jnp.bfloat16)
    for c in range(chan):
        for n in range(MODES):
            perm[c, n, n, c] = 1
    return perm.reshape(chan * MODES, MODES * chan)


def body(
    coords,
    features,
    valid_count,
    pair_block,
    pair_brick,
    pair_count,
    geometry,
    encoder_first,
    encoder_bias,
    encoder_second,
    decoder_first,
    decoder_bias,
    decoder_second,
    spectral,
    cotangent,
):
    subs = lax.axis_size("sub")
    devices = lax.axis_size("slab") * subs
    every = ("slab", "sub", "chan")
    slab_index = lax.axis_index("slab")
    sub_index = lax.axis_index("sub")
    chan_index = lax.axis_index("chan")
    pair = slab_index * subs + sub_index
    blocks_here = valid_count.shape[0]
    chan, planes, count_j, count_k = geometry.shape
    points = features.shape[0]
    hidden = encoder_first.shape[1]
    slots = subs * CAP
    cells = slots * BRICK
    all_cells = devices * cells
    own = spectral.shape[0] // 2
    rows = own * MODES
    split_n = MODES // own
    tab = {k: v if k.startswith("norm") else jnp.asarray(v) for k, v in
           tables(chan, planes, devices, count_j, count_k).items()}
    per_row = count_k // BRICK

    def place(values):
        return values // (count_j * per_row), values // per_row % count_j, values % per_row

    def make(refs):
        return Slots(refs, subs, planes, count_j, per_row)

    def shape(dims, kind=F32):
        return jax.ShapeDtypeStruct(dims, kind)

    def hold(*values):
        return lax.optimization_barrier(values)

    def ring(values, axis, size):
        moved = [values[0]]
        for k in range(1, size):
            moved.append(lax.ppermute(values[k], axis, [(i, (i + k) % size) for i in range(size)]))
        return moved

    scal = [(v, "scalar") for v in (pair_block, pair_brick, pair_count, valid_count)]
    features_t, cotangent_t = features.T, cotangent.T
    enc_layers = [encoder_first, encoder_bias[None], encoder_second.T]
    dec_layers = [decoder_first, decoder_bias[None], decoder_second.T]
    wide = BRICK * hidden
    by_slot = (max(1, slots // 4), 0)
    whole = "whole"
    w1_scratch = pltpu.VMEM((4, hidden, BLOCK), F32)
    hidden_shape = shape((slots * wide, BLOCK), BF16)
    values_shape = shape((chan, cells), BF16)

    def wholes(*arrays):
        return [(a, whole) for a in arrays]

    def net(sign, weight, keep, f, layers):
        outs = [(shape((slots * chan, wide), BF16), by_slot), (hidden_shape, by_slot)]
        if keep:
            outs += [(hidden_shape, by_slot), (shape((chan, cells)), whole)]
        else:
            outs += [(values_shape, whole)] * subs
        return call(
            functools.partial(net_kernel, sign, weight, keep, make),
            [*scal, *wholes(coords, f, *layers)], outs, [w1_scratch, pltpu.VMEM((wide, 128), BF16)],
        )

    with jax.named_scope("encoder_points"):
        enc_g, enc_slope, *message = net(1.0, QUADRATURE, False, features_t, enc_layers)
    with jax.named_scope("partial_exchange"):
        partials = ring(message, "sub", subs)

    slabs = devices // subs
    with jax.named_scope("slots_all"):
        pair_brick, _ = hold(pair_brick, message[0])
        around = jnp.stack(ring([pair_brick[0]] * slabs, "slab", slabs))
        bricks_all = jnp.take(around, (slab_index - jnp.arange(slabs)) % slabs, axis=0)
    lanes = chan * MODES
    with jax.named_scope("dense_transform"):
        dense, *latents = call(
            functools.partial(dense_kernel, subs, make),
            [*scal, *wholes(tab["fk"], tab["fjp"], *partials), (geometry, (planes, 1)),
             (tab["lh"], (1, 0)), (tab["ll"], (1, 0)), (jnp.asarray(permutation(chan)), (1, 0)),
             (tab["kc"], (1, 0))],
            [(shape((MODES * planes, lanes), BF16), whole), *[(values_shape, whole)] * subs],
            [pltpu.VMEM((planes * count_j, lanes), BF16)] * 2, 8e9, 1e7,
        )
    with jax.named_scope("dense_exchange"):
        dense = dense.reshape(MODES, planes, split_n, own * chan)
        dense = dense.transpose(0, 2, 1, 3).reshape(MODES * split_n, planes, own * chan)
        dense, pair = hold(dense, pair)
        dense = lax.all_to_all(dense, every, 0, 0, tiled=True)
        dense = dense.reshape(devices, 2, planes, own * chan)
        if planes % 8:
            dense = dense.transpose(1, 0, 2, 3).reshape(2, devices * planes, own * chan)
    with jax.named_scope("latent_exchange"):
        latents = ring(latents, "sub", subs)

    first_pair = (pair * 2 + chan_index) * own
    mode_j = first_pair // MODES
    kx = tab["kx"]
    norm_nl = jnp.asarray(tab["norm_nl"])
    if split_n > 1:
        begin = first_pair % MODES * MODES
        kx = lax.dynamic_slice_in_dim(kx, begin, rows, 0)
        norm_nl = lax.dynamic_slice_in_dim(norm_nl, begin, rows, 0)
    scale = norm_nl * lax.dynamic_index_in_dim(jnp.asarray(tab["norm_j"]), mode_j, 0, keepdims=False)
    scale_column, scale_row = scale[:, None], scale[None, :]
    fj = lax.dynamic_slice_in_dim(tab["fj"], mode_j, 1, 0)
    fj = jnp.broadcast_to(fj, (16, fj.shape[1]))
    layer, row, column = place(bricks_all)
    slab_of = jnp.arange(slabs, dtype=jnp.int32)[:, None, None, None]
    owner = jnp.arange(subs, dtype=jnp.int32)[None, None, :, None]
    plane = (slab_of * subs + owner) * planes + layer
    lines = jnp.stack([plane.reshape(-1), row.reshape(-1), column.reshape(-1) * BRICK])
    lines = jnp.repeat(lines, BRICK, axis=1)
    inner = jnp.arange(all_cells, dtype=jnp.int32) % BRICK
    rows_all = (lines + jnp.stack([0 * inner, 0 * inner, inner])).astype(F32)

    with jax.named_scope("cell_basis"):
        (bt,) = call(
            basis_kernel,
            wholes(rows_all, kx, tab["ix"][:rows], fj),
            [(shape((rows, all_cells), BF16), (all_cells // 256, 1))], [], 5e9, 8e6,
        )

    readers = shape((2 * devices, chan, cells), BF16)
    by_mode = shape((2 * chan, rows))
    mode_scratch = [
        pltpu.VMEM((rows, 128), F32),
        pltpu.VMEM((rows, 128), F32),
        pltpu.VMEM((4 * chan, rows), BF16),
        pltpu.VMEM((own, MODES, 2 * chan, 2 * chan), BF16),
        pltpu.SemaphoreType.DMA((min(8, own),)),
    ]
    core = chan_index.astype(jnp.int32).reshape(1)
    with jax.named_scope("mix"):
        bt, *latents = hold(bt, *latents)
        sent, coefficient = call(
            mix_kernel,
            [(core, "scalar"), *wholes(dense, tab["fi"], scale_row), (spectral, "raw"), (bt, (1, 0))],
            [(readers, whole), (by_mode, whole)], mode_scratch, 4e9, 2e7,
        )
    with jax.named_scope("preact_exchange"):
        arrived = lax.all_to_all(sent, every, 0, 0, tiled=True)
    swap = [(0, 1), (1, 0)]
    with jax.named_scope("coefficient_swap"):
        coef_near = lax.dynamic_slice_in_dim(coefficient, chan_index * chan, chan, 0)
        coef_sent = lax.dynamic_slice_in_dim(coefficient, (1 - chan_index) * chan, chan, 0)
        coef_far = lax.ppermute(coef_sent, "chan", swap)

    with jax.named_scope("decoder_points"):
        cotangent_t, _ = hold(cotangent_t, sent)
        dec_g, dec_slope, dec_hid, read_grads = net(
            -1.0, 1.0 / BRICK, True, cotangent_t, dec_layers
        )

    with jax.named_scope("cell_values"):
        arrived, read_grads, coef_far = hold(arrived, read_grads, coef_far)
        cell_grads, bricks = call(
            functools.partial(point_kernel, subs),
            wholes(arrived, read_grads, *latents),
            [(readers, whole), (shape((chan, cells)), whole)], [], 1e6, 1e6,
        )
    with jax.named_scope("cell_grads_all"):
        all_grads = lax.all_to_all(cell_grads, every, 0, 0, tiled=True)

    def back(sign, weight, decode, f, layers, operands, saved):
        outs = [(shape((devices, chan + 16, 2 * hidden), BF16), whole)]
        scratch = []
        if decode:
            outs = [(shape((chan + 16, hidden)), whole)]
            outs.append((shape((chan, points), BF16), whole))
            scratch.append(pltpu.VMEM((blocks_here, chan, BLOCK), F32))
        return call(
            functools.partial(back_kernel, sign, weight, decode, make),
            [*scal, *wholes(coords, f, layers[2], *operands),
             *[(v, by_slot) for v in saved]],
            outs, scratch,
        )

    with jax.named_scope("decoder_back"):
        dec_grads, decoded = back(
            -1.0, 1.0 / BRICK, True, cotangent_t, dec_layers, [bricks],
            [dec_g, dec_slope, dec_hid],
        )

    with jax.named_scope("mix_back"):
        all_grads, decoded = hold(all_grads, decoded)
        sent_back, grad_modes = call(
            mixback_kernel,
            [(core, "scalar"), *wholes(all_grads, scale_column, scale_row), (spectral, "raw"),
             (bt, (1, 0))],
            [(readers, whole), (by_mode, whole)],
            mode_scratch + [pltpu.VMEM((2 * chan, all_cells), BF16)], 4e9, 2e7,
        )
    with jax.named_scope("latent_grad_exchange"):
        arrived_back = lax.all_to_all(sent_back, every, 0, 0, tiled=True)
    with jax.named_scope("grad_swap"):
        grad_far = lax.ppermute(grad_modes, "chan", swap)
    with jax.named_scope("own_cells"):
        (own_grads,) = call(
            functools.partial(own_kernel, make),
            [*scal, *wholes(rows_all, all_grads)],
            [(shape((chan, cells)), whole)], [], 1e8, 1e6,
        )

    with jax.named_scope("grad_spectral"):
        block_n = min(8, own)
        steps = own // block_n
        width = block_n * MODES

        def lanes_spec(height):
            return pl.BlockSpec((height, width), lambda n, place: (0, n))

        def outer(half, coef, grad, held):
            more = [] if held is None else [held]
            return pl.pallas_call(
                outer_kernel,
                grid_spec=pltpu.PrefetchScalarGridSpec(
                    num_scalar_prefetch=1,
                    grid=(steps,),
                    in_specs=[lanes_spec(chan), lanes_spec(2 * chan)]
                    + [pl.BlockSpec(memory_space=pl.ANY)] * len(more),
                    out_specs=pl.BlockSpec(
                        (block_n, MODES, chan, 2 * chan),
                        lambda n, place: (place[0] * steps + n, 0, 0, 0),
                    ),
                    scratch_shapes=[pltpu.VMEM((16 * chan, 256), BF16)],
                ),
                out_shape=shape((2 * own, MODES, chan, 2 * chan), BF16),
                input_output_aliases={3: 0} if more else {},
                compiler_params=pltpu.CompilerParams(vmem_limit_bytes=VMEM_LIMIT),
                cost_estimate=pl.CostEstimate(
                    flops=10**7, bytes_accessed=10**7, transcendentals=0
                ),
            )(half, coef, grad, *more)

        grad_spectral = outer(core, coef_near, grad_modes, None)

    with jax.named_scope("encoder_back"):
        arrived_back, own_grads, grad_spectral = hold(arrived_back, own_grads, grad_spectral)
        (enc_grads,) = back(
            1.0, QUADRATURE, False, features_t, enc_layers, [own_grads, arrived_back, dec_grads],
            [enc_g, enc_slope],
        )
    with jax.named_scope("grad_spectral_far"):
        grad_far, _ = hold(grad_far, enc_grads)
        grad_spectral = outer(1 - core, coef_far, grad_far, grad_spectral)
    with jax.named_scope("weight_sums"):
        total = jnp.sum(
            lax.all_to_all(enc_grads, ("slab", "sub"), 0, 0, tiled=True).astype(F32), axis=0
        )
        small = total[chan : chan + 8]
        small = small + lax.ppermute(small, "chan", swap)
    enc_second = total[:chan, :hidden].T
    dec_second = total[:chan, hidden:].T
    return (
        decoded.T,
        small[0:3, :hidden],
        small[3, :hidden],
        enc_second,
        small[0:3, hidden:],
        small[3, hidden:],
        dec_second,
        grad_spectral,
    )


def solution(mesh):
    placed = (
        P(None, ("groups", "slab", "sub")),
        P(("groups", "slab", "sub"), "chan"),
        P(("groups", "slab", "sub")),
        P(("groups", "slab"), None, None, None),
        P(("groups", "slab"), None, None, None),
        P(("groups", "slab"), None, None),
        P("chan", ("groups", "slab", "sub"), None, None),
        P(),
        P(),
        P(None, "chan"),
        P(),
        P(),
        P(None, "chan"),
        P(("slab", "sub"), None, None, None),
        P(("groups", "slab", "sub"), "chan"),
    )
    return jax.shard_map(
        body,
        mesh=mesh,
        in_specs=placed,
        out_specs=(
            P(("groups", "slab", "sub"), "chan"),
            P("groups", None),
            P("groups"),
            P("groups", "chan"),
            P("groups", None),
            P("groups"),
            P("groups", "chan"),
            P(("groups", "slab", "sub"), None, "chan", None),
        ),
        check_vma=False,
    )
```
